128 devices in a mesh: dp: 16 (over z, x_hi, core), tensor: 8 (over x_lo, y).
Axes of the slice: x: 4 (x_hi: 2, x_lo: 2; x = x_hi * 2 + x_lo), y: 4, z: 4, core: 2. Of those that a mesh axis runs over, the one named last changes fastest.
Arguments:
- resid_in: bfloat16 [32768, 768], P(('dp', 'tensor')), may hold values from -6 to 6
- cotangent: bfloat16 [32768, 768], P(('dp', 'tensor')), may hold values from -6 to 6
- segments: int32 [32768], P('dp'), may hold values from 0 to 3, as said below
- in_gain: float32 [768], replicated, may hold values from 0.5 to 1.5
- w_gate: bfloat16 [768, 1536], P('dp', 'tensor'), may hold values from -0.21875 to 0.21875
- w_value: bfloat16 [768, 1536], P('dp', 'tensor'), may hold values from -0.21875 to 0.21875
- w_step: bfloat16 [768, 24], P('dp', 'tensor'), may hold values from -0.21875 to 0.21875
- w_shared: bfloat16 [768, 256], replicated, may hold values from -0.21875 to 0.21875
- conv_inner: float32 [4, 1536], P(None, 'tensor'), may hold values from -0.5 to 0.5
- bias_inner: float32 [1536], P('tensor'), may hold values from -0.5 to 0.5
- conv_shared: float32 [4, 256], replicated, may hold values from -0.5 to 0.5
- bias_shared: float32 [256], replicated, may hold values from -0.5 to 0.5
- step_bias: float32 [24], P('tensor'), may hold values from -3 to -2
- decay_log: float32 [24], P('tensor'), may hold values from -9 to -0.8
- skip_gain: float32 [24], P('tensor'), may hold values from 0.5 to 1.5
- out_gain: float32 [1536], P('tensor'), may hold values from 0.5 to 1.5
- w_out: bfloat16 [768, 1536], P('dp', 'tensor'), may hold values from -0.15625 to 0.15625
Outputs:
- result: bfloat16 [32768, 768], P(('dp', 'tensor'))
- grad_resid: float32 [32768, 768], P(('dp', 'tensor'))
- grad_in_gain: float32 [768], replicated
- grad_w_gate: float32 [768, 1536], P('dp', 'tensor')
- grad_w_value: float32 [768, 1536], P('dp', 'tensor')
- grad_w_step: float32 [768, 24], P('dp', 'tensor')
- grad_w_shared: float32 [768, 256], replicated
- grad_conv_inner: float32 [4, 1536], P(None, 'tensor')
- grad_bias_inner: float32 [1536], P('tensor')
- grad_conv_shared: float32 [4, 256], replicated
- grad_bias_shared: float32 [256], replicated
- grad_step_bias: float32 [24], P('tensor')
- grad_decay_log: float32 [24], P('tensor')
- grad_skip_gain: float32 [24], P('tensor')
- grad_out_gain: float32 [1536], P('tensor')
- grad_w_out: float32 [768, 1536], P('dp', 'tensor')
The draws below stay inside these ranges and needn't reach their ends.
Inputs may be any that keep to these rules, and one draw needn't show every extreme that they name: `segments`: each sequence holds four documents numbered 0 to 3 in order, each of 256 tokens or more.
All inputs are finite; a program needn't handle non-finite values.
Results may differ from the reference program's by a relative error of at most 0.022.
Values may be sent and summed in bfloat16 or wider, within the bound.
A program may use at most 128 MiB of HBM per device.

```python
import jax
import jax.numpy as jnp
from jax import lax

D = 768
HEADS = 24
HEADDIM = 64
STATE = 128
CONV = 4
GROUP = 256
INNER = 1536
LEN = 2048
SEQUENCES = 16
TOKENS = 32768


def draw_segments(key, part):
    key = jax.random.fold_in(key, 11)
    least = LEN // 8
    most = LEN * 9 // 32
    pieces = jax.random.randint(key, (SEQUENCES, 3), least, most + 1)
    first = pieces[:, 0]
    second = first + pieces[:, 1]
    third = second + pieces[:, 2]
    places = jnp.arange(LEN, dtype=jnp.int32)[None, :]
    ident = (places >= first[:, None]).astype(jnp.int32)
    ident = ident + (places >= second[:, None]).astype(jnp.int32)
    ident = ident + (places >= third[:, None]).astype(jnp.int32)
    return ident.reshape(TOKENS)


def draw_decay_log(key, part):
    key = jax.random.fold_in(key, 23)
    share = jax.random.uniform(key, (HEADS,), jnp.float32)
    bottom = 0.2 / LEN
    upper = 0.05
    rate = jnp.exp(jnp.log(bottom) + share * (jnp.log(upper) - jnp.log(bottom)))
    return jnp.log(rate / 0.12)


def steps_of(stream_key, dims, shards, low, high):
    def one(position, parts):
        draws = jax.random.uniform(jax.random.fold_in(jax.random.fold_in(stream_key, 6), position), (parts,), jnp.float32, low / len(shards), high / len(shards))
        return jnp.repeat(jnp.exp(draws), dims[position] // parts).reshape((-1,) + (1,) * (len(dims) - position - 1))

    factor_of = one(*shards[0])
    for cut in shards[1:]:
        factor_of = factor_of * one(*cut)
    return factor_of


def centred(stream_key, shape, scale, limit, shards=(), held_as=jnp.bfloat16):
    drawn = jax.random.normal(stream_key, shape, jnp.float32) * scale
    if len(shards) > 0:
        drawn = steps_of(stream_key, shape, shards, -0.22, 0.18) * drawn
    return jnp.clip(drawn, min=-limit, max=limit).astype(held_as)


def setup_inputs(seed: int = 0) -> dict:
    splits = jax.random.split(jax.random.key(seed), 18)
    return {
        "resid_in": centred(splits[0], (TOKENS, D), 1.0, 6.0, ((0, 128),)),
        "cotangent": centred(splits[1], (TOKENS, D), 1.0, 6.0, ((0, 128),)),
        "segments": draw_segments(jax.random.fold_in(splits[17], 71), 0),
        "in_gain": jnp.clip(1.0 + 0.1 * jax.random.normal(splits[3], (D,), jnp.float32), 0.5, 1.5),
        "w_gate": centred(splits[4], (D, INNER), D ** -0.5, 0.21875, ((0, 16), (1, 8))),
        "w_value": centred(splits[5], (D, INNER), D ** -0.5, 0.21875, ((0, 16), (1, 8))),
        "w_step": centred(splits[6], (D, HEADS), D ** -0.5, 0.21875, ((0, 16), (1, 8))),
        "w_shared": centred(splits[7], (D, 2 * STATE), D ** -0.5, 0.21875),
        "conv_inner": jnp.clip(jax.random.uniform(splits[8], (CONV, INNER), jnp.float32, -0.5, 0.5) * steps_of(splits[8], (CONV, INNER), ((1, 8),), -0.4, 0.0), -0.5, 0.5),
        "bias_inner": jnp.clip(jax.random.uniform(splits[9], (INNER,), jnp.float32, -0.5, 0.5) * steps_of(splits[9], (INNER,), ((0, 8),), -0.4, 0.0), -0.5, 0.5),
        "conv_shared": jnp.clip(jax.random.uniform(splits[10], (CONV, 2 * STATE), jnp.float32, -0.5, 0.5), -0.5, 0.5),
        "bias_shared": jnp.clip(jax.random.uniform(splits[11], (2 * STATE,), jnp.float32, -0.5, 0.5), -0.5, 0.5),
        "step_bias": jnp.clip(-3.0 + 1.0 * jax.random.uniform(splits[12], (HEADS,), jnp.float32) ** steps_of(splits[12], (HEADS,), ((0, 8),), -0.2, 0.2), -3.0, -2.0),
        "decay_log": draw_decay_log(jax.random.fold_in(splits[17], 71), 0),
        "skip_gain": jnp.clip(0.5 + 1.0 * jax.random.uniform(splits[14], (HEADS,), jnp.float32) ** steps_of(splits[14], (HEADS,), ((0, 8),), -0.2, 0.2), 0.5, 1.5),
        "out_gain": jnp.clip(1.0 + 0.1 * jax.random.normal(splits[15], (INNER,), jnp.float32), 0.5, 1.5),
        "w_out": centred(splits[16], (D, INNER), INNER ** -0.5, 0.15625, ((0, 16), (1, 8))),
    }


HIGHEST = lax.Precision.HIGHEST
EPSILON = 1e-05

@jax.custom_vjp
def low(v):
    return lax.optimization_barrier(v.astype(jnp.bfloat16)).astype(jnp.float32)

@jax.custom_vjp
def low_back(v):
    return v

def low_keep(v):
    return (low(v), None)

def low_pass(kept, grad):
    return (grad,)

def back_keep(v):
    return (v, None)

def back_low(kept, grad):
    return (low(grad),)
low.defvjp(low_keep, low_pass)
low_back.defvjp(back_keep, back_low)

def causal_conv(before, weight, offset, segment):
    taps, channels = weight.shape
    summed = offset[None, :] + weight[taps - 1][None, :] * before
    for back in range(1, taps):
        shifted = jnp.concatenate([jnp.zeros((back, channels), before.dtype), before[:-back]], 0)
        earlier = jnp.concatenate([jnp.full((back,), -1, jnp.int32), segment[:-back]], 0)
        usable = (earlier == segment)[:, None]
        summed = summed + weight[taps - 1 - back][None, :] * jnp.where(usable, shifted, 0.0)
    return jax.nn.silu(summed)

def block_scan(values, bees, cees, step_values, step_offset, decay, skip, segment):
    length, heads, width = values.shape
    blocks = length // GROUP
    steps = jax.nn.softplus(step_values + step_offset[None, :])
    rates = steps * (-jnp.exp(decay))[None, :]

    def split(array):
        return array.reshape((blocks, GROUP) + array.shape[1:])
    causal = jnp.arange(GROUP)[:, None] >= jnp.arange(GROUP)[None, :]

    def advance(carry, block):
        state, last_id = carry
        vals, bmat, cmat, step_blk, rate_blk, ident = block
        logs = jnp.cumsum(rate_blk.T, axis=1)
        allowed = (causal & (ident[:, None] == ident[None, :]))[None]
        gaps = logs[:, :, None] - logs[:, None, :]
        decays = jnp.where(allowed, jnp.exp(jnp.where(allowed, gaps, 0.0)), 0.0)
        scores = jnp.dot(cmat, bmat.T, precision=HIGHEST)
        mixing = scores[None] * decays * step_blk.T[:, None, :]
        inside = jnp.einsum('hts,shp->thp', mixing, vals, precision=HIGHEST)
        joined = (ident == last_id)[None, :]
        carried = jnp.where(joined, jnp.exp(logs), 0.0)
        from_state = jnp.einsum('tn,hnp->thp', cmat, state, precision=HIGHEST) * carried.T[:, :, None]
        ending = (ident == ident[-1])[None, :]
        weights = jnp.where(ending, jnp.exp(logs[:, -1:] - logs), 0.0) * step_blk.T
        fresh = jnp.einsum('sn,hs,shp->hnp', bmat, weights, vals, precision=HIGHEST)
        kept = jnp.where(ident[-1] == last_id, jnp.exp(logs[:, -1]), 0.0)
        state = fresh + state * kept[:, None, None]
        return ((state, ident[-1]), inside + from_state)
    start = (jnp.zeros((heads, bees.shape[1], width), values.dtype), jnp.int32(-1))
    ignored, outputs = lax.scan(jax.checkpoint(advance), start, (split(values), split(bees), split(cees), split(steps), split(rates), split(segment)))
    return outputs.reshape(length, heads, width) + skip[None, :, None] * values

def block_forward(segment, inputs, in_gain, w_gate, w_value, w_step, w_shared, conv_inner, bias_inner, conv_shared, bias_shared, step_bias, decay_log, skip_gain, out_gain, w_out):
    length = inputs.shape[0]
    mean_sq = lax.optimization_barrier(jnp.mean(inputs * inputs, axis=1, keepdims=True))
    scaled = inputs * lax.rsqrt(mean_sq + EPSILON)
    normed = low(scaled * in_gain[None, :])
    gate_pre = low_back(jnp.dot(normed, w_gate, precision=HIGHEST))
    value_pre = low_back(jnp.dot(normed, w_value, precision=HIGHEST))
    step_raw = low_back(jnp.dot(normed, w_step, precision=HIGHEST))
    shared_pre = low_back(jnp.dot(normed, w_shared, precision=HIGHEST))
    values = low(causal_conv(value_pre, conv_inner, bias_inner, segment))
    shared = low(causal_conv(shared_pre, conv_shared, bias_shared, segment))
    mixed = block_scan(values.reshape(length, HEADS, HEADDIM), shared[:, :STATE], shared[:, STATE:], step_raw, step_bias, decay_log, skip_gain, segment).reshape(length, INNER)
    gated = mixed * jax.nn.silu(gate_pre)
    inverse = lax.rsqrt(lax.optimization_barrier(jnp.mean(gated * gated, axis=1, keepdims=True)) + EPSILON)
    normed_out = low(gated * inverse * out_gain[None, :])
    return inputs + jnp.dot(normed_out, w_out.T, precision=HIGHEST)

def reference(resid_in, cotangent, segments, in_gain, w_gate, w_value, w_step, w_shared, conv_inner, bias_inner, conv_shared, bias_shared, step_bias, decay_log, skip_gain, out_gain, w_out):
    params = tuple((param.astype(jnp.float32) for param in (in_gain, w_gate, w_value, w_step, w_shared, conv_inner, bias_inner, conv_shared, bias_shared, step_bias, decay_log, skip_gain, out_gain, w_out)))
    rows_in = resid_in.astype(jnp.float32).reshape(SEQUENCES, LEN, D)
    rows_cot = cotangent.astype(jnp.float32).reshape(SEQUENCES, LEN, D)
    ids_all = segments.reshape(SEQUENCES, LEN)

    def visit(totals, item):
        sequence, seq_cot, seq_ids = item

        def forward(inputs, *weights):
            return block_forward(seq_ids, inputs, *weights)
        output, pullback = jax.vjp(forward, sequence, *params)
        grads = pullback(seq_cot)
        totals = tuple((total + grad for total, grad in zip(totals, grads[1:])))
        return (totals, (output.astype(jnp.bfloat16), grads[0]))
    start = tuple((jnp.zeros_like(param) for param in params))
    totals, (outputs, grad_in) = lax.scan(visit, start, (rows_in, rows_cot, ids_all))
    return (outputs.reshape(TOKENS, D), grad_in.reshape(TOKENS, D), totals[0], totals[1], totals[2], totals[3], totals[4], totals[5], totals[6], totals[7], totals[8], totals[9], totals[10], totals[11], totals[12], totals[13])
```

```python
import jax
import jax.numpy as jnp
from jax import lax
from jax.experimental import pallas as pl
from jax.experimental.pallas import tpu as pltpu
from jax.sharding import PartitionSpec as P

D = 768
HEADS = 24
HEADDIM = 64
STATE = 128
INNER = 1536
ROWS = 256
HALO = 16
PARTS = 8
WIDE = 192
PACK = 640
EPSILON = 1e-05
VMEM_LIMIT = 60 * 1024 * 1024
MESH = pl.DeviceIdType.MESH
HIGHEST = lax.Precision.HIGHEST
F32 = jnp.float32
BF16 = jnp.bfloat16

ORDERS = (("x", "y", "z"), ("y", "z", "x"), ("z", "x", "y"))
DIMS = ("x", "y", "z")


def place():
    dp, tensor = lax.axis_index("dp"), lax.axis_index("tensor")
    x = (dp // 2 % 2) * 2 + tensor // 4
    return {"x": x, "y": tensor % 4, "z": dp // 4, "core": dp % 2}


def device_of(at):
    return (at["z"] * 4 + (at["x"] // 2) * 2 + at["core"], (at["x"] % 2) * 4 + at["y"])


def moved(me, dim, by):
    return {**me, dim: (me[dim] + by) % 4}


def sibling(me):
    return {**me, "core": 1 - me["core"]}


def region(fixed):
    free = slice(None)
    x_lo, x_hi = (fixed["x"] % 2, fixed["x"] // 2) if "x" in fixed else (free, free)
    return (x_lo, fixed.get("y", free), fixed.get("z", free), x_hi)


def free_shape(fixed):
    sizes = (("x", 2), ("y", 4), ("z", 4), ("x", 2))
    return tuple(size for dim, size in sizes if dim not in fixed)


def greet(me):
    barrier = pltpu.get_barrier_semaphore()
    others = [moved(me, dim, by) for dim in DIMS for by in (1, 2, 3)] + [sibling(me)]
    for other in others:
        pl.semaphore_signal(barrier, inc=1, device_id=device_of(other), device_id_type=MESH)
    pl.semaphore_wait(barrier, len(others))


def send(src, dst, sems, slot, target):
    send_sem, recv_sem = sems
    copy = pltpu.make_async_remote_copy(
        src_ref=src,
        dst_ref=dst,
        send_sem=send_sem.at[slot],
        recv_sem=recv_sem.at[slot],
        device_id=device_of(target),
        device_id_type=MESH,
    )
    copy.start()
    return copy


def spread(me, own, buf, sems, base):
    core = me["core"]
    pending = []

    def part(p, dims):
        return buf.at[region({dim: me[dim] for dim in dims}) + (core, p)]

    def along(p, stage, src, dst):
        dim = ORDERS[p][stage]
        return [
            send(src, dst, sems, base + p * 13 + stage * 3 + by - 1, moved(me, dim, by))
            for by in (1, 3, 2)
        ]

    def across(p, value, step):
        piece = buf.at[region({ORDERS[p][2]: value}) + (core, p)]
        pending.append(send(piece, piece, sems, base + p * 13 + 9 + step, sibling(me)))

    started = [along(p, 0, own(p), part(p, ORDERS[p])) for p in range(3)]
    for stage in (1, 2):
        following = []
        for p in range(3):
            for copy in started[p]:
                copy.wait_recv()
            pending.extend(started[p])
            piece = part(p, ORDERS[p][stage:])
            following.append((along(p, stage, piece, piece)))
        for p in range(3):
            for copy in started[p]:
                copy.wait_send()
        pending = [copy for copy in pending if all(copy is not c for s in started for c in s)]
        started = following
    for p in range(3):
        across(p, me[ORDERS[p][2]], 0)
    for order, by in enumerate((1, 3, 2)):
        for p in range(3):
            started[p][order].wait_recv()
            across(p, (me[ORDERS[p][2]] - by) % 4, by)
    for p in range(3):
        for copy in started[p]:
            copy.wait_send()
    for copy in pending:
        copy.wait()


GATHER_SEMS = 39


def gather_kernel(w_ref, out_ref, send_sem, recv_sem, local_sem):
    me = place()
    greet(me)
    here = region({dim: me[dim] for dim in DIMS}) + (me["core"],)
    keep = pltpu.make_async_copy(w_ref, out_ref.at[here], local_sem)
    keep.start()
    keep.wait()
    spread(me, lambda p: w_ref.at[p], out_ref, (send_sem, recv_sem), 0)


def gather_weights(block):
    out = pl.pallas_call(
        gather_kernel,
        out_shape=jax.ShapeDtypeStruct((2, 4, 4, 2, 2, 3, 16, PACK), BF16),
        in_specs=[pl.BlockSpec(memory_space=pl.ANY)],
        out_specs=pl.BlockSpec(memory_space=pl.ANY),
        scratch_shapes=[
            pltpu.SemaphoreType.DMA((GATHER_SEMS,)),
            pltpu.SemaphoreType.DMA((GATHER_SEMS,)),
            pltpu.SemaphoreType.DMA,
        ],
        compiler_params=pltpu.CompilerParams(collective_id=0, has_side_effects=True),
    )(block.reshape(3, 16, PACK))
    return out.reshape(PARTS, D, PACK)


TAIL = 128


def reduce_kernel(
    part_ref, small_ref, out_ref, tail_ref, small_out,
    own, heard, got_c, got_b, got_a, sum_c, sum_b, tail, small_got, small_sum,
    send_sem, recv_sem, small_send, small_recv, local_sem, tail_send, tail_recv,
):
    me = place()
    core = me["core"]
    greet(me)
    sems = (send_sem, recv_sem)
    small_sems = (small_send, small_recv)
    steps = (1, 3, 2, 0)
    copies = {}
    waiting = []

    def last(p, by):
        dim = ORDERS[p][2]
        return {dim: (me[dim] + by) % 4}

    for by in steps:
        for p in range(3):
            there = region(last(p, by))
            copies[p, by] = (
                send(part_ref.at[there + (1 - core, p)], heard[p].at[by], sems, p * 13 + by, sibling(me)),
                pltpu.make_async_copy(part_ref.at[there + (core, p)], own[p].at[by], local_sem.at[p * 4 + by]),
            )
            copies[p, by][1].start()
    small_copy = send(small_ref, small_got.at[9], small_sems, 9, sibling(me))

    onward = {}
    for by in steps:
        for p in range(3):
            remote, local = copies[p, by]
            local.wait()
            remote.wait_recv()
            own[p][by] = own[p][by] + heard[p][by]
            if by:
                onward[p, by] = send(
                    own[p].at[by], got_c[p].at[by - 1], sems, p * 13 + 4 + by - 1, moved(me, ORDERS[p][2], by)
                )
    small_copy.wait()
    small_sum[0] = small_ref[...] + small_got[9]

    def small_send_along(stage, dim):
        return [
            send(small_sum.at[stage], small_got.at[stage * 3 + by - 1], small_sems, stage * 3 + by - 1, moved(me, dim, by))
            for by in (1, 3, 2)
        ]

    def small_add(stage, sent):
        for copy in sent:
            copy.wait_recv()
        waiting.extend(sent)
        base = stage * 3
        total = (small_sum[stage] + small_got[base]) + (small_got[base + 1] + small_got[base + 2])
        if stage < 2:
            small_sum[stage + 1] = total
        else:
            small_out[...] = total

    small_sent = small_send_along(0, "z")
    for p in range(3):
        for by in (1, 3, 2):
            onward[p, by].wait_recv()
        got = got_c[p]
        sum_c[p][...] = (
            (own[p][0].astype(F32) + got[0].astype(F32)) + (got[1].astype(F32) + got[2].astype(F32))
        ).astype(BF16)
    small_add(0, small_sent)
    small_sent = small_send_along(1, "y")

    second = {}
    for p in range(3):
        dim, fixed = ORDERS[p][1], ORDERS[p][2]
        for by in (1, 3, 2):
            second[p, by] = send(
                sum_c[p].at[inner_index(p, dim, (me[dim] + by) % 4)],
                got_b[p].at[by - 1], sems, p * 13 + 7 + by - 1, moved(me, dim, by),
            )
    for p in range(3):
        dim = ORDERS[p][1]
        for by in (1, 3, 2):
            second[p, by].wait_recv()
        got = got_b[p]
        mine = sum_c[p][inner_index(p, dim, me[dim])]
        sum_b[p][...] = (
            (mine.astype(F32) + got[0].astype(F32)) + (got[1].astype(F32) + got[2].astype(F32))
        ).astype(BF16)
    small_add(1, small_sent)
    small_sent = small_send_along(2, "x")

    third = {}
    for p in range(3):
        dim = ORDERS[p][0]
        for by in (1, 3, 2):
            third[p, by] = send(
                sum_b[p].at[line_index(p, dim, (me[dim] + by) % 4)],
                got_a.at[p, by - 1], sems, p * 13 + 10 + by - 1, moved(me, dim, by),
            )
    for p in range(3):
        dim = ORDERS[p][0]
        for by in (1, 3, 2):
            third[p, by].wait_recv()
        mine = sum_b[p][line_index(p, dim, me[dim])].astype(F32)
        total = (mine + got_a[p, 0].astype(F32)) + (got_a[p, 1].astype(F32) + got_a[p, 2].astype(F32))
        out_ref[p] = total
        tail[p] = total[:, PACK - TAIL:].astype(BF16)
    small_add(2, small_sent)

    here = region({dim: me[dim] for dim in DIMS}) + (core,)
    keep = pltpu.make_async_copy(tail, tail_ref.at[here], local_sem.at[12])
    keep.start()
    keep.wait()
    spread(me, lambda p: tail.at[p], tail_ref, (tail_send, tail_recv), 0)

    for remote, local in copies.values():
        remote.wait_send()
    for copy in list(onward.values()) + list(second.values()) + list(third.values()) + waiting:
        copy.wait_send()


def inner_index(p, dim, value):
    full = region({dim: value})
    fixed = ORDERS[p][2]
    return tuple(i for i, name in zip(full, ("x", "y", "z", "x")) if name != fixed)


def line_index(p, dim, value):
    full = region({dim: value})
    return tuple(i for i, name in zip(full, ("x", "y", "z", "x")) if name == dim)


def reduce_grads(parts, small):
    big = parts.reshape(2, 4, 4, 2, 2, 3, 16, PACK)
    block = (16, PACK)

    def shapes(lead, stage):
        return [pltpu.VMEM(lead + free_shape(ORDERS[p][stage:]) + block, BF16) for p in range(3)]

    def body(part_ref, small_ref, out_ref, tail_ref, small_out, *rest):
        groups = [rest[i * 3 : i * 3 + 3] for i in range(2)]
        rest = rest[6:]
        got_c, rest = rest[:3], rest[3:]
        got_b, rest = rest[:3], rest[3:]
        got_a, rest = rest[0], rest[1:]
        sum_c, rest = rest[:3], rest[3:]
        sum_b, rest = rest[:3], rest[3:]
        reduce_kernel(part_ref, small_ref, out_ref, tail_ref, small_out, groups[0], groups[1], got_c, got_b, got_a, sum_c, sum_b, *rest)

    rows = small.shape[0]
    dma = pltpu.SemaphoreType.DMA
    out, tail, total = pl.pallas_call(
        body,
        out_shape=(
            jax.ShapeDtypeStruct((3, 16, PACK), F32),
            jax.ShapeDtypeStruct((2, 4, 4, 2, 2, 3, 16, TAIL), BF16),
            jax.ShapeDtypeStruct((rows, 128), F32),
        ),
        in_specs=[pl.BlockSpec(memory_space=pl.ANY), pl.BlockSpec(memory_space=pltpu.VMEM)],
        out_specs=(
            pl.BlockSpec(memory_space=pltpu.VMEM),
            pl.BlockSpec(memory_space=pl.ANY),
            pl.BlockSpec(memory_space=pltpu.VMEM),
        ),
        scratch_shapes=[
            *shapes((4,), 2), *shapes((4,), 2), *shapes((3,), 2), *shapes((3,), 1),
            pltpu.VMEM((3, 3) + block, BF16),
            *shapes((), 2), *shapes((), 1),
            pltpu.VMEM((3, 16, TAIL), BF16),
            pltpu.VMEM((10, rows, 128), F32),
            pltpu.VMEM((3, rows, 128), F32),
            dma((39,)), dma((39,)), dma((10,)), dma((10,)), dma((13,)),
            dma((GATHER_SEMS,)), dma((GATHER_SEMS,)),
        ],
        compiler_params=pltpu.CompilerParams(
            collective_id=1, has_side_effects=True, vmem_limit_bytes=VMEM_LIMIT
        ),
    )(big, small)
    return out.reshape(48, PACK), tail.reshape(PARTS, D, TAIL), total


def dot(a, b, over_a, over_b, precision=None):
    return lax.dot_general(
        a, b, (((over_a,), (over_b,)), ((), ())), precision=precision, preferred_element_type=F32
    )


def head_lanes():
    head = lax.broadcasted_iota(jnp.int32, (128, INNER), 0)
    unit = lax.broadcasted_iota(jnp.int32, (128, INNER), 1)
    return jnp.where(unit // HEADDIM == head, 1.0, 0.0).astype(BF16)


def halves(v):
    top = v.astype(BF16)
    return top, (v - top.astype(F32)).astype(BF16)


def to_units(v, spread_heads):
    top, rest = halves(v)
    return dot(top, spread_heads, 1, 0) + dot(rest, spread_heads, 1, 0)


def to_heads(v, spread_heads):
    top, rest = halves(v)
    return dot(top, spread_heads, 1, 1) + dot(rest, spread_heads, 1, 1)


def lower_triangle():
    row = lax.broadcasted_iota(jnp.int32, (ROWS, ROWS), 0)
    return row >= lax.broadcasted_iota(jnp.int32, (ROWS, ROWS), 1)


def conv_sum(before, taps, bias, same):
    total = bias + taps[3:4] * before[HALO:]
    for back in (1, 2, 3):
        total = total + taps[3 - back : 4 - back] * (same[:, back : back + 1] * before[HALO - back : HALO - back + ROWS])
    return total


def silu_slope(v):
    sig = jax.nn.sigmoid(v)
    return sig * (1.0 + v * (1.0 - sig))


def step_weights(w_ref):
    total = w_ref[0, :, PACK - 128 :]
    for t in range(1, PARTS):
        total = total + w_ref[t, :, PACK - 128 :]
    return total


def enter_kernel(
    x_ref, gain_ref, w_ref, wsh_ref, prm_ref, hp_ref, csh_ref, bsh_ref, same_ref, ends_ref,
    normed_ref, gate_ref, vpre_ref, vsum_ref, val_ref, spre_ref, ssum_ref, bc_ref,
    raw_ref, dt_ref, logs_ref, fresh_ref,
):
    x = x_ref[...].astype(F32)
    inverse = lax.rsqrt(jnp.mean(x * x, axis=1, keepdims=True) + EPSILON)
    normed = (x * inverse * gain_ref[...]).astype(BF16)
    normed_ref[...] = normed[HALO:]
    same = same_ref[...]
    for t in range(PARTS):
        cols = slice(t * WIDE, (t + 1) * WIDE)
        both = dot(normed, w_ref[t, :, : 2 * WIDE], 1, 0)
        gate_ref[:, cols] = both[HALO:, :WIDE]
        before = both[:, WIDE:]
        vpre_ref[:, cols] = before
        total = conv_sum(before, prm_ref[0:4, cols], prm_ref[4:5, cols], same)
        vsum_ref[:, cols] = total
        val_ref[:, cols] = (total * jax.nn.sigmoid(total)).astype(BF16)
    before = dot(normed, wsh_ref[...], 1, 0)
    spre_ref[...] = before
    total = conv_sum(before, csh_ref[...], bsh_ref[...], same)
    ssum_ref[...] = total
    bc_ref[...] = (total * jax.nn.sigmoid(total)).astype(BF16)

    step = dot(normed[HALO:], step_weights(w_ref), 1, 0)
    is_head = lax.broadcasted_iota(jnp.int32, (ROWS, 128), 1) < HEADS
    raw = jnp.where(is_head, pltpu.roll(step, 64, 1) + hp_ref[0:1], 0.0)
    raw_ref[...] = raw
    dt = jnp.where(is_head, jnp.maximum(raw, 0.0) + jnp.log1p(jnp.exp(-jnp.abs(raw))), 0.0)
    dt_ref[...] = dt
    logs = dot(lower_triangle().astype(F32), dt * hp_ref[1:2], 1, 0, HIGHEST)
    logs_ref[...] = logs
    lanes = head_lanes()
    last = logs[ROWS - 1 :]
    ends = ends_ref[...]
    weights = ends[:, 0:1] * jnp.exp(last - logs) * dt
    weighted = (val_ref[...].astype(F32) * to_units(weights, lanes)).astype(BF16)
    fresh_ref[0:STATE] = dot(bc_ref[:, :STATE], weighted, 0, 0).astype(BF16)
    kept = to_units(ends[0:8, 2:3] * jnp.exp(jnp.broadcast_to(last, (8, 128))), lanes)
    top, rest = halves(kept[0:1])
    row = lax.broadcasted_iota(jnp.int32, (16, INNER), 0)
    fresh_ref[STATE:] = jnp.where(row == 0, top.astype(F32), jnp.where(row == 1, rest.astype(F32), 0.0)).astype(BF16)


def middle_kernel(
    x_ref, cot_ref, w_ref, prm_ref, hp_ref, gate_ref, val_ref, bc_ref, dt_ref, logs_ref,
    state_ref, ends_ref, ids_ref,
    result_ref, nout_ref, dgate_ref, dval_ref, dscore_ref, dstate_ref, dlog_ref, direct_ref, rows_ref,
    mix_ref, dec_ref, mixed_ref, inner_ref, dout_ref, dy_ref,
):
    lanes = head_lanes()
    ends = ends_ref[...]
    logs, dt = logs_ref[...], dt_ref[...]
    logs_t, dt_t = logs.T, dt.T
    bmat, cmat = bc_ref[:, :STATE], bc_ref[:, STATE:]
    allowed = lower_triangle() & (ends[:, 3:4] == ids_ref[...])
    scores = jnp.where(allowed, dot(cmat, bmat, 1, 1), 0.0)
    carried = to_units(ends[:, 1:2] * jnp.exp(logs), lanes)
    state = state_ref[...]
    inner_ref[...] = dot(cmat, state, 1, 0) * carried
    first_half = lax.broadcasted_iota(jnp.int32, (ROWS, 128), 1) < HEADDIM

    def pair(ref, tile):
        both = ref[:, tile * 128 : tile * 128 + 128]
        zero = jnp.zeros_like(both)
        return jnp.where(first_half, both, zero), jnp.where(first_half, zero, both)

    for tile in range(HEADS // 2):
        cols = slice(tile * 128, tile * 128 + 128)
        total = inner_ref[:, cols]
        for h, vals in zip((2 * tile, 2 * tile + 1), pair(val_ref, tile)):
            gaps = jnp.minimum(logs[:, h : h + 1] - logs_t[h : h + 1], 0.0)
            decay = jnp.exp(gaps) * dt_t[h : h + 1]
            dec_ref[h] = decay.astype(BF16)
            mix = (scores * decay).astype(BF16)
            mix_ref[h] = mix
            total = total + dot(mix, vals, 1, 0)
        inner_ref[:, cols] = total

    mixed = inner_ref[...] + to_units(hp_ref[2:10], lanes)[0:1] * val_ref[...].astype(F32)
    mixed_ref[...] = mixed
    gate = gate_ref[...]
    sig = jax.nn.sigmoid(gate)
    gated = mixed * (gate * sig)
    inverse = lax.rsqrt(jnp.sum(gated * gated, axis=1, keepdims=True) / INNER + EPSILON)
    out_gain = prm_ref[5:6]
    nout_ref[...] = (gated * inverse * out_gain).astype(BF16)
    cot = cot_ref[...]
    branch = x_ref[...].astype(F32)
    for t in range(PARTS):
        cols = slice(t * WIDE, (t + 1) * WIDE)
        w_out = w_ref[t, :, 2 * WIDE : 3 * WIDE]
        branch = branch + dot(nout_ref[:, cols], w_out, 1, 1)
        dout_ref[:, cols] = dot(cot, w_out, 1, 0)
    result_ref[...] = branch.astype(BF16)

    d_out = dout_ref[...]
    normal = gated * inverse
    rows_ref[0:1] = jnp.sum(d_out * normal, axis=0, keepdims=True)
    d_scaled = d_out * out_gain
    dot_total = jnp.sum(d_scaled * normal, axis=1, keepdims=True)
    d_gated = inverse * (d_scaled - normal * (dot_total / INNER))
    d_mixed = d_gated * (gate * sig)
    dgate_ref[...] = (d_gated * mixed * sig * (1.0 + gate * (1.0 - sig))).astype(BF16)
    vals = val_ref[...].astype(F32)
    rows_ref[1:2] = jnp.sum(d_mixed * vals, axis=0, keepdims=True)
    dy_ref[...] = d_mixed.astype(BF16)
    dval_ref[...] = to_units(hp_ref[2:10], lanes)[0:1] * d_mixed

    d_scores = jnp.zeros((ROWS, ROWS), F32)
    dlog = jnp.zeros((ROWS, 128), F32)
    direct = jnp.zeros((ROWS, 128), F32)
    for tile in range(HEADS // 2):
        cols = slice(tile * 128, tile * 128 + 128)
        total = jnp.zeros((ROWS, 128), F32)
        for h, vals, grads in zip((2 * tile, 2 * tile + 1), pair(val_ref, tile), pair(dy_ref, tile)):
            d_mix = dot(grads, vals, 1, 1)
            d_scores = d_scores + d_mix * dec_ref[h].astype(F32)
            total = total + dot(mix_ref[h], grads, 0, 0)
        dval_ref[:, cols] = dval_ref[:, cols] + total
        from_values = total * val_ref[:, cols].astype(F32)
        dout_ref[:, cols] = from_values
    from_values = dout_ref[...]
    direct_ref[...] = to_heads(from_values, lanes)
    dlog_ref[...] = to_heads(dy_ref[...].astype(F32) * inner_ref[...] - from_values, lanes)
    d_scores = jnp.where(allowed, d_scores, 0.0).astype(BF16)
    d_carried = (dy_ref[...].astype(F32) * carried).astype(BF16)
    dscore_ref[:, :STATE] = dot(d_scores, cmat, 0, 0)
    dscore_ref[:, STATE:] = dot(d_scores, bmat, 1, 0) + dot(d_carried, state, 1, 1)
    dstate_ref[...] = dot(cmat, d_carried, 0, 0).astype(BF16)


def leave_kernel(
    val_ref, bc_ref, raw_ref, dt_ref, logs_ref, state_ref, coming_ref, ends_ref, hp_ref,
    dval_ref, dscore_ref, dlog_ref, direct_ref, vpre_ref, vsum_ref, spre_ref, ssum_ref, same_ref,
    dsum_ref, dssum_ref, dstep_ref, heads_ref, rows_ref, srows_ref,
):
    lanes = head_lanes()
    ends = ends_ref[...]
    logs, dt, raw = logs_ref[...], dt_ref[...], raw_ref[...]
    bmat = bc_ref[:, :STATE]
    coming = coming_ref[...]
    last = logs[ROWS - 1 :]
    weights = to_units(ends[:, 0:1] * jnp.exp(last - logs) * dt, lanes)
    vals = val_ref[...].astype(F32)
    weighted = vals * weights
    below = dot(bmat, coming, 1, 0)
    d_values = dval_ref[...] + weights * below
    through = to_heads(weighted * below, lanes)
    d_bees = dscore_ref[:, :STATE] + dot(weighted.astype(BF16), coming, 1, 1)
    kept = ends[0:8, 2:3] * jnp.exp(jnp.broadcast_to(last, (8, 128)))
    held = jnp.sum(coming.astype(F32) * state_ref[...].astype(F32), axis=0, keepdims=True)
    d_kept = to_heads(jnp.broadcast_to(held, (8, INNER)), lanes)
    d_last = jnp.sum(through, axis=0, keepdims=True) + (d_kept * kept)[0:1]
    upper = (lax.broadcasted_iota(jnp.int32, (ROWS, ROWS), 0) <= lax.broadcasted_iota(jnp.int32, (ROWS, ROWS), 1))
    d_rate = dot(upper.astype(F32), dlog_ref[...] - through, 1, 0, HIGHEST) + d_last
    by_rate = dt * hp_ref[1:2] * d_rate
    slope = jnp.where(raw < -15.0, 1.0, jax.nn.sigmoid(raw) / jnp.where(raw < -15.0, 1.0, dt))
    is_head = lax.broadcasted_iota(jnp.int32, (ROWS, 128), 1) < HEADS
    d_step = jnp.where(is_head, (direct_ref[...] + through + by_rate) * slope, 0.0)
    dstep_ref[...] = d_step.astype(BF16)
    heads_ref[...] = jnp.zeros_like(heads_ref)
    heads_ref[0:1] = jnp.sum(d_step, axis=0, keepdims=True)
    heads_ref[1:2] = jnp.sum(by_rate, axis=0, keepdims=True)
    same = same_ref[...]

    def conv_grads(d_sum, before_ref, out_ref):
        out_ref[3:4] = jnp.sum(d_sum * before_ref[HALO:], axis=0, keepdims=True)
        out_ref[4:5] = jnp.sum(d_sum, axis=0, keepdims=True)
        for back in (1, 2, 3):
            shifted = same[:, back : back + 1] * before_ref[HALO - back : HALO - back + ROWS]
            out_ref[3 - back : 4 - back] = jnp.sum(d_sum * shifted, axis=0, keepdims=True)

    d_sum = d_values * silu_slope(vsum_ref[...])
    dsum_ref[...] = d_sum
    rows_ref[...] = jnp.zeros_like(rows_ref)
    conv_grads(d_sum, vpre_ref, rows_ref)
    d_sum = jnp.concatenate([d_bees, dscore_ref[:, STATE:]], axis=1) * silu_slope(ssum_ref[...])
    dssum_ref[...] = d_sum
    srows_ref[...] = jnp.zeros_like(srows_ref)
    conv_grads(d_sum, spre_ref, srows_ref)


def close_kernel(
    x_ref, cot_ref, gain_ref, normed_ref, nout_ref, w_ref, wsh_ref, prm_ref, csh_ref,
    dgate_ref, dsum_ref, dssum_ref, next_ref, snext_ref, dstep_ref, after_ref,
    resid_ref, parts_ref, rows_ref, dval_ref,
):
    after = after_ref[...]

    def conv_back(d_sum, following, taps):
        joined = jnp.concatenate([d_sum, following], axis=0)
        total = taps[3:4] * d_sum
        for ahead in (1, 2, 3):
            total = total + taps[3 - ahead : 4 - ahead] * (after[:, ahead : ahead + 1] * joined[ahead : ahead + ROWS])
        return total.astype(BF16)

    dval_ref[...] = conv_back(dsum_ref[...], next_ref[...], prm_ref[0:4])
    d_shared = conv_back(dssum_ref[...], snext_ref[...], csh_ref[...])
    normed_t = normed_ref[...].T
    cot = cot_ref[...]
    cot_t = cot.T
    dstep = dstep_ref[...]
    step_part = dot(normed_t, dstep, 1, 0)[:, :32].astype(BF16)
    shared_part = dot(normed_t, d_shared, 1, 0).astype(BF16)
    d_normed = dot(pltpu.roll(dstep.astype(F32), 64, 1).astype(BF16), step_weights(w_ref), 1, 1)
    d_normed = d_normed + dot(d_shared, wsh_ref[...], 1, 1)
    for t in range(PARTS):
        cols = slice(t * WIDE, (t + 1) * WIDE)
        both = jnp.concatenate([dgate_ref[:, cols], dval_ref[:, cols]], axis=1)
        parts_ref[t, :, : 2 * WIDE] = dot(normed_t, both, 1, 0).astype(BF16)
        outs = dot(cot_t, nout_ref[:, cols], 1, 0).astype(BF16)
        parts_ref[t, :, 2 * WIDE :] = jnp.concatenate([outs, step_part, shared_part[:, t * 32 : t * 32 + 32]], axis=1)
        d_normed = d_normed + dot(both, w_ref[t, :, : 2 * WIDE], 1, 1)
    x = x_ref[...].astype(F32)
    inverse = lax.rsqrt(jnp.mean(x * x, axis=1, keepdims=True) + EPSILON)
    scaled = x * inverse
    d_in = d_normed * gain_ref[...]
    rows_ref[...] = jnp.sum(d_normed * scaled, axis=0, keepdims=True)
    centred = jnp.mean(d_in * scaled, axis=1, keepdims=True)
    resid_ref[...] = inverse * (d_in - scaled * centred) + cot.astype(F32)


def call(kernel, outs, args, scratch=()):
    return pl.pallas_call(
        kernel,
        out_shape=tuple(jax.ShapeDtypeStruct(shape, dtype) for shape, dtype in outs),
        in_specs=[pl.BlockSpec(memory_space=pltpu.VMEM)] * len(args),
        out_specs=tuple(pl.BlockSpec(memory_space=pltpu.VMEM) for _ in outs),
        scratch_shapes=list(scratch),
        compiler_params=pltpu.CompilerParams(vmem_limit_bytes=VMEM_LIMIT),
    )(*args)


def by_heads(blocks):
    rows = blocks.shape[0]
    pieces = blocks.reshape(rows, PARTS, WIDE).transpose(1, 0, 2)
    return lax.all_to_all(pieces, "tensor", split_axis=0, concat_axis=0, tiled=True)


def by_blocks(pieces):
    back = lax.all_to_all(pieces, "tensor", split_axis=0, concat_axis=0, tiled=True)
    return back.transpose(1, 0, 2).reshape(pieces.shape[1], INNER)


def shards(
    resid_in, cotangent, segments, in_gain, w_gate, w_value, w_step, w_shared, conv_inner, bias_inner,
    conv_shared, bias_shared, step_bias, decay_log, skip_gain, out_gain, w_out,
):
    tensor = lax.axis_index("tensor")
    heads_local = w_step.shape[1]

    extra = lax.dynamic_update_slice(
        jnp.zeros((w_step.shape[0], PACK - 3 * WIDE), BF16), w_step, (jnp.int32(0), tensor * heads_local)
    )
    weights = gather_weights(jnp.concatenate([w_gate, w_value, w_out, extra], axis=1))
    per_head = jnp.stack([step_bias, decay_log, skip_gain])
    own_prm = jnp.concatenate([conv_inner, bias_inner[None], out_gain[None]], axis=0)
    own_prm = jnp.concatenate(
        [own_prm, jnp.pad(per_head.reshape(1, -1), ((0, 0), (0, WIDE - 9))), jnp.zeros((1, WIDE), F32)], axis=0
    )
    all_prm = lax.all_gather(own_prm, "tensor", axis=0)
    prm = all_prm.transpose(1, 0, 2).reshape(8, INNER)
    heads = all_prm[:, 6, :9].reshape(PARTS, 3, heads_local).transpose(1, 0, 2).reshape(3, HEADS)
    heads = jnp.stack([heads[0], -jnp.exp(heads[1]), heads[2]])
    hp = jnp.pad(heads, ((0, 13), (0, 128 - HEADS)))

    ring = [(i, (i + 1) % PARTS) for i in range(PARTS)]
    ahead = lax.ppermute(resid_in[ROWS - HALO :], "tensor", ring)
    tokens = jnp.concatenate([ahead, resid_in], axis=0)
    padded = jnp.concatenate([jnp.full((8,), -1, jnp.int32), segments, jnp.full((8,), -1, jnp.int32)])
    around = lax.dynamic_slice(padded, (tensor * ROWS,), (ROWS + 16,))
    ids = around[8 : 8 + ROWS]
    lanes8 = lambda columns: jnp.stack(columns + [jnp.zeros((ROWS,), F32)] * (8 - len(columns)), axis=1)
    same = lanes8([jnp.ones((ROWS,), F32)] + [(around[8 - k : 8 - k + ROWS] == ids).astype(F32) for k in (1, 2, 3)])
    after = lanes8([jnp.ones((ROWS,), F32)] + [(around[8 + k : 8 + k + ROWS] == ids).astype(F32) for k in (1, 2, 3)])
    before, last = around[7], ids[ROWS - 1]
    ends = lanes8([
        (ids == last).astype(F32), (ids == before).astype(F32),
        jnp.broadcast_to((last == before).astype(F32), (ROWS,)), ids.astype(F32),
    ])
    ids_row = ids.astype(F32)[None]

    big, small, heads_f = (ROWS, INNER), (ROWS, 2 * STATE), (ROWS, 128)
    normed, gate, vpre, vsum, vals, spre, ssum, bc, raw, dt, logs, fresh = call(
        enter_kernel,
        [
            ((ROWS, D), BF16), (big, F32), ((ROWS + HALO, INNER), F32), (big, F32), (big, BF16),
            ((ROWS + HALO, 2 * STATE), F32), (small, F32), (small, BF16),
            (heads_f, F32), (heads_f, F32), (heads_f, F32), ((STATE + 16, INNER), BF16),
        ],
        (tokens, in_gain[None], weights, w_shared, prm, hp, conv_shared, bias_shared[None], same, ends),
    )

    arrived = by_heads(fresh).astype(F32)
    kept = arrived[:, STATE] + arrived[:, STATE + 1]
    state, states = jnp.zeros((STATE, WIDE), F32), []
    for block in range(PARTS):
        states.append(state.astype(BF16))
        state = arrived[block, :STATE] + kept[block][None] * state
    state = by_blocks(jnp.stack(states))

    result, nout, dgate, dval, dscore, dstate, dlog, direct, rows_out = call(
        middle_kernel,
        [
            ((ROWS, D), BF16), (big, BF16), (big, BF16), (big, F32), (small, F32), ((STATE, INNER), BF16),
            (heads_f, F32), (heads_f, F32), ((8, INNER), F32),
        ],
        (resid_in, cotangent, weights, prm, hp, gate, vals, bc, dt, logs, state, ends, ids_row),
        [
            pltpu.VMEM((HEADS, ROWS, ROWS), BF16), pltpu.VMEM((HEADS, ROWS, ROWS), BF16),
            pltpu.VMEM(big, F32), pltpu.VMEM(big, F32), pltpu.VMEM(big, F32), pltpu.VMEM(big, BF16),
        ],
    )

    arrived = by_heads(dstate).astype(F32)
    coming, comings = jnp.zeros((STATE, WIDE), F32), [None] * PARTS
    for block in reversed(range(PARTS)):
        comings[block] = coming.astype(BF16)
        coming = arrived[block] + kept[block][None] * coming
    coming = by_blocks(jnp.stack(comings))

    dsum, dssum, dstep, head_rows, rows_conv, srows_conv = call(
        leave_kernel,
        [
            (big, F32), (small, F32), (heads_f, BF16), ((8, 128), F32), ((8, INNER), F32), ((8, 2 * STATE), F32),
        ],
        (
            vals, bc, raw, dt, logs, state, coming, ends, hp, dval, dscore, dlog, direct,
            vpre, vsum, spre, ssum, same,
        ),
    )
    back_ring = [(i, (i - 1) % PARTS) for i in range(PARTS)]
    following = lax.ppermute(jnp.concatenate([dsum[:8], dssum[:8]], axis=1), "tensor", back_ring)
    grad_resid, parts, rows_in = call(
        close_kernel,
        [((ROWS, D), F32), ((PARTS, D, PACK), BF16), ((1, D), F32)],
        (
            resid_in, cotangent, in_gain[None], normed, nout, weights, w_shared, prm, conv_shared, dgate,
            dsum, dssum, following[:, :INNER], following[:, INNER:], dstep, after,
        ),
        [pltpu.VMEM(big, BF16)],
    )

    pieces = [
        rows_conv[:5], rows_out[:2], srows_conv[:5], head_rows[:2], rows_in,
    ]
    flat = jnp.concatenate([piece.reshape(-1) for piece in pieces])
    rows = -(-flat.size // 1024) * 8
    flat = jnp.pad(flat, (0, rows * 128 - flat.size)).reshape(rows, 128)
    block, tails, flat = reduce_grads(parts, flat)
    flat = flat.reshape(-1)
    sums, at = [], 0
    for piece in pieces:
        sums.append(flat[at : at + piece.size].reshape(piece.shape))
        at += piece.size
    inner_rows, out_rows, shared_rows, head_sums, gain_row = sums
    mine = lambda row: lax.dynamic_slice_in_dim(row, tensor * WIDE, WIDE, axis=-1)
    own_heads = lambda row: lax.dynamic_slice_in_dim(row, tensor * heads_local, heads_local, axis=-1)
    grad_w_shared = tails[:, :, TAIL - 32 :].transpose(1, 0, 2).reshape(D, 2 * STATE).astype(F32)
    return (
        result,
        grad_resid,
        gain_row[0],
        block[:, :WIDE],
        block[:, WIDE : 2 * WIDE],
        own_heads(block[:, 3 * WIDE : 3 * WIDE + HEADS]),
        grad_w_shared,
        mine(inner_rows[:4]),
        mine(inner_rows[4]),
        shared_rows[:4],
        shared_rows[4],
        own_heads(head_sums[0]),
        own_heads(head_sums[1]),
        mine(out_rows[1]).reshape(heads_local, HEADDIM).sum(axis=1),
        mine(out_rows[0]),
        block[:, 2 * WIDE : 3 * WIDE],
    )


def solution(mesh):
    rows, cols = P(("dp", "tensor"), None), P("dp", "tensor")
    head, whole = P("tensor"), P()
    in_specs = (
        rows, rows, P("dp"), whole, cols, cols, cols, whole, P(None, "tensor"), head,
        whole, whole, head, head, head, head, cols,
    )
    out_specs = (
        rows, rows, whole, cols, cols, cols, whole, P(None, "tensor"), head,
        whole, whole, head, head, head, head, cols,
    )
    return jax.shard_map(shards, mesh=mesh, in_specs=in_specs, out_specs=out_specs, check_vma=False)
```

```python
import types

import jax
import jax.numpy as jnp
from jax import lax
from jax.experimental import pallas as pl
from jax.experimental.pallas import tpu as pltpu
from jax.sharding import PartitionSpec as P

D = 768
HEADS = 24
HEADDIM = 64
STATE = 128
INNER = 1536
ROWS = 256
HALO = 16
PARTS = 8
WIDE = 192
PACK_V = 256
PACK_G = 384
EPSILON = 1e-05
VMEM_LIMIT = 62 * 1024 * 1024
MESH = pl.DeviceIdType.MESH
HIGHEST = lax.Precision.HIGHEST
F32 = jnp.float32
BF16 = jnp.bfloat16

ORDERS = (("x", "y", "z"), ("y", "z", "x"), ("z", "x", "y"))
DIMS = ("x", "y", "z")
ASIDE = (("x", "y", "z"), ("y", "x", "z"), ("z", "y", "x"))
EVERY = slice(None)


def place():
    dp, tensor = lax.axis_index("dp"), lax.axis_index("tensor")
    x = (dp // 2 % 2) * 2 + tensor // 4
    return {"x": x, "y": tensor % 4, "z": dp // 4, "core": dp % 2, "dp": dp, "t": tensor}


def device_of(at):
    return (at["z"] * 4 + (at["x"] // 2) * 2 + at["core"], (at["x"] % 2) * 4 + at["y"])


def moved(me, dim, by):
    return {**me, dim: (me[dim] + by) % 4}


def sibling(me):
    return {**me, "core": 1 - me["core"]}


def region(fixed, half=None):
    x_lo, x_hi = (fixed["x"] % 2, fixed["x"] // 2) if "x" in fixed else (EVERY, EVERY)
    y, z = fixed.get("y", EVERY), fixed.get("z", EVERY)
    if half is not None:
        if "x" not in fixed:
            x_lo = pl.ds(half, 1)
        else:
            y = pl.ds(half * 2, 2)
    return (x_lo, y, z, x_hi)


def free_shape(fixed, half=False):
    sizes = [[dim, size] for dim, size in (("x", 2), ("y", 4), ("z", 4), ("x", 2)) if dim not in fixed]
    if half:
        sizes[0][1] //= 2
    return tuple(size for dim, size in sizes)


def transfer(src, dst, sems, slot, target):
    copy = pltpu.make_async_remote_copy(
        src_ref=src,
        dst_ref=dst,
        send_sem=sems[0].at[slot],
        recv_sem=sems[1].at[slot],
        device_id=target,
        device_id_type=MESH,
    )
    copy.start()
    return copy


def send(src, dst, sems, slot, target):
    return transfer(src, dst, sems, slot, device_of(target))


def peer(me, step):
    z_x = (me["z"] * 2 + me["x"] // 2 + step // 8) % 8
    return (z_x * 2 + me["core"], (me["t"] + step % 8) % 8)


def each_peer(body):
    def step(i, carry):
        body(i)
        return carry

    lax.fori_loop(1, 64, step, 0)


def neighbours(me):
    along = [device_of(moved(me, dim, by)) for dim in DIMS for by in (1, 2, 3)]
    return along + [device_of(sibling(me))] + [(me["dp"], ((me["t"] + 4) % 8 // 4) * 4 + (me["y"] + by) % 4) for by in (1, 2, 3)]


def greet(me):
    for other in neighbours(me):
        pl.semaphore_signal(pltpu.get_barrier_semaphore(), inc=1, device_id=other, device_id_type=MESH)


def greeted():
    pl.semaphore_wait(pltpu.get_barrier_semaphore(), 13)


GATHER_SLOTS = 15
REDUCE_SLOTS = 14


class Gather:
    def __init__(self, me, own, buf, sems, relayed):
        self.me, self.own, self.buf, self.sems, self.relayed = me, own, buf, sems, relayed
        self.sent, self.got = [], {}

    def unit(self, p, stage, value, half=None):
        order = ORDERS[p]
        fixed = {dim: self.me[dim] for dim in order[stage + 1 :]}
        fixed[order[stage]] = value
        return self.buf.at[region(fixed, half) + (self.me["core"], p)]

    def go(self, name, p, slot, piece, target, source=None):
        copy = send(piece if source is None else source, piece, self.sems, p * GATHER_SLOTS + slot, target)
        self.sent.append(copy)
        self.got[name, p] = copy

    def first(self):
        me = self.me
        for p in range(3):
            dim = ORDERS[p][0]
            for by in (1, 3, 2):
                self.go(("a", by), p, by - 1, self.unit(p, 0, me[dim]), moved(me, dim, by), self.own.at[p])
        here = region({dim: me[dim] for dim in DIMS}) + (me["core"],)
        self.buf[here] = self.own[...]

    def second(self):
        me = self.me
        for p in range(3):
            for by in (1, 3, 2):
                self.got[("a", by), p].wait_recv()
            dim = ORDERS[p][1]
            for by in (1, 3, 2):
                self.go(("b", by), p, 2 + by, self.unit(p, 1, me[dim]), moved(me, dim, by))

    def third(self):
        me = self.me
        for p in range(3):
            for by in (1, 3, 2):
                self.got[("b", by), p].wait_recv()
            dim = ORDERS[p][2]
            unit = self.unit(p, 2, me[dim])
            self.go(("c", 1), p, 6, unit, moved(me, dim, 1))
            self.go(("c", 3), p, 7, unit, moved(me, dim, 3))
            if not self.relayed:
                self.go(("c", 2), p, 8, unit, moved(me, dim, 2))
        for p in range(3):
            self.across(p, 10, me[ORDERS[p][2]])

    def across(self, p, slot, value, half=None):
        self.go(("s", slot), p, slot, self.unit(p, 2, value, half), sibling(self.me))

    def relay(self):
        me = self.me
        for p in range(3):
            dim = ORDERS[p][2]
            for step, by, half in ((1, 1, 0), (3, 3, 1)):
                self.got[("c", by), p].wait_recv()
                value = (me[dim] - by) % 4
                if self.relayed:
                    self.go(("r", half), p, 8 + half, self.unit(p, 2, value, half), moved(me, dim, by))
                self.across(p, 11 + half, value)

    def finish(self):
        me = self.me
        for p in range(3):
            across = (me[ORDERS[p][2]] + 2) % 4
            if self.relayed:
                for half in (0, 1):
                    self.got[("r", half), p].wait_recv()
                    self.across(p, 13 + half, across, half)
            else:
                self.got[("c", 2), p].wait_recv()
                self.across(p, 13, across)

    def settle(self):
        for p in range(3):
            for slot in (10, 11, 12, 13, 14) if self.relayed else (10, 11, 12, 13):
                self.got[("s", slot), p].wait_recv()

    def drain(self):
        for copy in self.sent:
            copy.wait_send()


class Reduce:
    def __init__(self, me, orders, parts, heard, relayed, got_c, got_b, got_a, sems):
        self.me, self.orders, self.parts, self.sems = me, orders, parts, sems
        self.heard, self.relayed, self.got_c, self.got_b, self.got_a = heard, relayed, got_c, got_b, got_a
        self.sent, self.got = [], {}

    def unit(self, p, stage, by, half=None):
        order = self.orders[p]
        fixed = {dim: self.me[dim] for dim in order[stage + 1 :]}
        fixed[order[stage]] = (self.me[order[stage]] + by) % 4
        return region(fixed, half)

    def mine(self, p, stage, by, half=None):
        return self.unit(p, stage, by, half) + (self.me["core"], p)

    def go(self, name, p, slot, src, dst, target):
        copy = send(src, dst, self.sems, p * REDUCE_SLOTS + slot, target)
        self.sent.append(copy)
        self.got[name, p] = copy

    def swap(self):
        me = self.me
        for by in (2, 1, 3, 0):
            for p in range(3):
                src = self.parts.at[self.unit(p, 2, by) + (1 - me["core"], p)]
                self.go(("s", by), p, by, src, self.heard[p].at[by], sibling(me))

    def heard_add(self, by):
        for p in range(3):
            self.got[("s", by), p].wait_recv()
            at = self.mine(p, 2, by)
            self.parts[at] = self.parts[at] + self.heard[p][by]

    def relay(self):
        for by in (2, 1, 3):
            self.heard_add(by)
            for p in range(3):
                dim = self.orders[p][2]
                if self.relayed is None:
                    src, dst = self.parts.at[self.mine(p, 2, by)], self.got_c[p].at[by - 1]
                    self.go(("c", by), p, 3 + by, src, dst, moved(self.me, dim, by))
                elif by == 2:
                    for to, half in ((1, 0), (3, 1)):
                        src = self.parts.at[self.mine(p, 2, 2, half)]
                        self.go(("r", half), p, 4 + half, src, self.relayed[p].at[half], moved(self.me, dim, to))

    def third(self):
        for p in range(3):
            dim = self.orders[p][2]
            for by, half in ((1, 0), (3, 1)):
                if self.relayed is not None:
                    self.got[("r", half), p].wait_recv()
                    at = self.mine(p, 2, by, half)
                    self.parts[at] = self.parts[at] + self.relayed[p][half]
                    src = self.parts.at[self.mine(p, 2, by)]
                    self.go(("c", by), p, 6 + half, src, self.got_c[p].at[half], moved(self.me, dim, by))
        self.heard_add(0)

    def second(self):
        for p in range(3):
            for by in (1, 3) if self.relayed is not None else (1, 3, 2):
                self.got[("c", by), p].wait_recv()
            at, got = self.mine(p, 2, 0), self.got_c[p]
            summed = self.parts[at].astype(F32) + (got[0].astype(F32) + got[1].astype(F32))
            if self.relayed is None:
                summed = summed + got[2].astype(F32)
            self.parts[at] = summed.astype(BF16)
            dim = self.orders[p][1]
            for by in (1, 3, 2):
                self.go(("b", by), p, 7 + by, self.parts.at[self.mine(p, 1, by)], self.got_b[p].at[by - 1], moved(self.me, dim, by))

    def first(self):
        for p in range(3):
            for by in (1, 3, 2):
                self.got[("b", by), p].wait_recv()
            at, got = self.mine(p, 1, 0), self.got_b[p]
            self.parts[at] = (
                (self.parts[at].astype(F32) + got[0].astype(F32)) + (got[1].astype(F32) + got[2].astype(F32))
            ).astype(BF16)
            dim = self.orders[p][0]
            for by in (1, 3, 2):
                self.go(("a", by), p, 10 + by, self.parts.at[self.mine(p, 0, by)], self.got_a.at[p, by - 1], moved(self.me, dim, by))

    def result(self, p):
        for by in (1, 3, 2):
            self.got[("a", by), p].wait_recv()
        got = self.got_a
        return (self.parts[self.mine(p, 0, 0)].astype(F32) + got[p, 0].astype(F32)) + (
            got[p, 1].astype(F32) + got[p, 2].astype(F32)
        )

    def drain(self):
        for copy in self.sent:
            copy.wait_send()


class Total:
    def __init__(self, me, own, sums, got, sems):
        self.me, self.own, self.sums, self.got, self.sems = me, own, sums, got, sems
        self.sent = []

    def along(self, stage):
        me, src = self.me, self.own if stage == 0 else self.sums.at[stage - 1]
        if stage == 0:
            peers = [(9, sibling(me))]
        else:
            dim = DIMS[3 - stage]
            peers = [((stage - 1) * 3 + by - 1, moved(me, dim, by)) for by in (1, 3, 2)]
        self.now = [send(src, self.got.at[slot], self.sems, slot, peer) for slot, peer in peers]
        self.sent += self.now

    def add(self, stage):
        for copy in self.now:
            copy.wait_recv()
        got = self.got
        if stage == 0:
            self.sums[0] = self.own[...] + got[9]
        else:
            base = (stage - 1) * 3
            self.sums[stage] = (self.sums[stage - 1] + got[base]) + (got[base + 1] + got[base + 2])

    def drain(self):
        for copy in self.sent:
            copy.wait_send()


class Shared:
    def __init__(self, me, tiles, heard, got, own, tails, sems):
        self.me, self.tiles, self.heard, self.got, self.own, self.tails = me, tiles, heard, got, own, tails
        self.sems = sems
        self.sent = []

    def at(self, device):
        return (device[0] // 4, device[0] // 2 % 2, device[0] % 2, device[1])

    def here(self):
        return self.at((self.me["dp"], self.me["t"]))

    def half(self, core):
        return (EVERY, EVERY, core)

    def across(self, src, dst, slot):
        copy = send(src, dst, self.sems, slot, sibling(self.me))
        self.sent.append(copy)
        return copy

    def swap(self):
        self.swapped = self.across(self.tiles.at[self.half(1 - self.me["core"])], self.heard, 0)

    def everyone(self, src, dst, slot):
        def go(i):
            to = peer(self.me, i)
            pltpu.make_async_remote_copy(
                src_ref=src(to), dst_ref=dst, send_sem=self.sems[0].at[slot], recv_sem=self.sems[1].at[slot],
                device_id=to, device_id_type=MESH,
            ).start()

        each_peer(go)

    def wait(self, kind, slot):
        all_tiles = self.got.at[pl.ds(0, 63)]
        pltpu.make_async_copy(all_tiles, all_tiles, self.sems[kind].at[slot]).wait()

    def scatter(self):
        self.swapped.wait_recv()
        mine = self.half(self.me["core"])
        self.tiles[mine] = self.tiles[mine] + self.heard[...]
        z, x_hi, _, t = self.here()
        place = (z * 2 + x_hi) * 8 + t
        self.everyone(lambda to: self.tiles.at[self.at(to)], self.got.at[place], 1)
        self.got[place] = self.tiles[self.here()]

    def gather(self):
        self.wait(1, 1)
        total = jnp.sum(self.got[...].astype(F32), axis=0).astype(BF16)
        self.own[...] = total
        self.everyone(lambda to: self.own, self.tails.at[self.here()], 2)
        self.tails[self.here()] = total

    def share(self):
        self.wait(1, 2)
        mine = self.tails.at[self.half(self.me["core"])]
        self.shared = self.across(mine, mine, 3)

    def finish(self):
        self.shared.wait_recv()

    def drain(self):
        self.wait(0, 1)
        self.wait(0, 2)
        for copy in self.sent:
            copy.wait_send()


class Swap:
    def __init__(self, me, src, got, sems):
        self.me, self.src, self.got, self.sems = me, src, got, sems
        self.copies = []

    def start(self):
        dp, t = self.me["dp"], self.me["t"]
        for by in (4, 2, 6, 1, 7, 3, 5):
            to = (t + by) % PARTS
            self.copies.append(transfer(self.src.at[to], self.got.at[t], self.sems, by, (dp, to)))
        self.got[t] = self.src[t]

    def wait(self):
        for copy in self.copies:
            copy.wait_recv()

    def drain(self):
        for copy in self.copies:
            copy.wait_send()


def dot(a, b, over_a, over_b, precision=None):
    return lax.dot_general(
        a, b, (((over_a,), (over_b,)), ((), ())), precision=precision, preferred_element_type=F32
    )


def head_lanes():
    head = lax.broadcasted_iota(jnp.int32, (128, INNER), 0)
    unit = lax.broadcasted_iota(jnp.int32, (128, INNER), 1)
    low = head * HEADDIM
    return jnp.where((unit >= low) & (unit < low + HEADDIM), 1.0, 0.0).astype(BF16)


def halves(v):
    top = v.astype(BF16)
    return top, (v - top.astype(F32)).astype(BF16)


def to_units(v, lanes):
    top, rest = halves(v)
    return dot(top, lanes, 1, 0) + dot(rest, lanes, 1, 0)


def to_heads(v, lanes):
    top, rest = halves(v)
    return dot(top, lanes, 1, 1) + dot(rest, lanes, 1, 1)


def lower_triangle():
    row = lax.broadcasted_iota(jnp.int32, (ROWS, ROWS), 0)
    return row >= lax.broadcasted_iota(jnp.int32, (ROWS, ROWS), 1)


def first_half():
    return lax.broadcasted_iota(jnp.int32, (ROWS, 128), 1) < HEADDIM


def silu_slope(v):
    sig = jax.nn.sigmoid(v)
    return sig * (1.0 + v * (1.0 - sig))


def of_part(t):
    return slice(t * WIDE, (t + 1) * WIDE)


def weights_of(buf, t):
    block = buf[t // 4, t % 4]
    return block.reshape(D, block.shape[-1])


def pair(ref, cols, first):
    both = ref[:, cols]
    zero = jnp.zeros_like(both)
    return jnp.where(first, both, zero), jnp.where(first, zero, both)


def norm_of(x, gain):
    x = x.astype(F32)
    inverse = lax.rsqrt(jnp.mean(x * x, axis=1, keepdims=True) + EPSILON)
    return (x * inverse * gain).astype(BF16)


def pack(buf, whole):
    for k in range(PARTS):
        other, low = 8 + k // 2, k % 2 * 64
        buf[k, :STATE] = whole[:, k * 128 : k * 128 + 128]
        buf[k, STATE : STATE + 64] = whole[low : low + 64, other * 128 : other * 128 + 128]


def unpack(whole, buf):
    for k in range(PARTS):
        other, low = 8 + k // 2, k % 2 * 64
        whole[:, k * 128 : k * 128 + 128] = buf[k, :STATE]
        whole[low : low + 64, other * 128 : other * 128 + 128] = buf[k, STATE : STATE + 64]


def kept_of(s, block):
    rows = s.fresh_in[block, STATE + 64 :].astype(F32)
    first = lax.broadcasted_iota(jnp.int32, (STATE + 64, 128), 0) < STATE
    return jnp.where(first, rows[0:1] + rows[1:2], rows[2:3] + rows[3:4])


def make_blocks(s, me):
    t = me["t"]
    row = lax.broadcasted_iota(jnp.int32, (64, 48), 0)
    given = s.w_step[...].astype(F32)
    steps = jnp.zeros((64, 48), F32)
    for k in range(3):
        steps = jnp.where(row == 3 * t + k, given[k : k + 1], steps)
    s.turned[...] = jnp.zeros_like(s.turned)
    s.turned[:, :48] = steps
    steps = s.turned[...].T[:48].astype(BF16)
    for p in range(3):
        rows = slice(16 * p, 16 * p + 16)
        s.own_v[p, :, :WIDE] = s.w_value[rows]
        s.own_v[p, :, WIDE:] = steps[rows]
        s.own_g[p, :, :WIDE] = s.w_gate[rows]
        s.own_g[p, :, WIDE:] = s.w_out[rows]
    lane = lax.broadcasted_iota(jnp.int32, (1, 256), 1)
    row6, row7 = jnp.zeros((1, 256), F32), jnp.zeros((1, 256), F32)
    for k in range(3):
        row6 = jnp.where(lane == 3 * t + k, s.step_bias[k], row6)
        row6 = jnp.where(lane == 128 + 3 * t + k, s.decay_log[k], row6)
        row7 = jnp.where(lane == 3 * t + k, s.skip_gain[k], row7)
    s.own_p[...] = jnp.zeros_like(s.own_p)
    s.own_p[0:4, :WIDE] = s.conv_inner[...]
    s.own_p[4:5, :WIDE] = s.bias_inner[...].reshape(1, WIDE)
    s.own_p[5:6, :WIDE] = s.out_gain[...].reshape(1, WIDE)
    s.own_p[6:7] = row6
    s.own_p[7:8] = row7


SAME, AFTER, ENDING, JOINED, KEPT, IDS = 0, 3, 7, 8, 9, 10


def segs_of(s, block):
    return s.segs[pl.ds(pl.multiple_of(block * ROWS, ROWS), ROWS)].reshape(1, ROWS).astype(F32)


def make_masks(s, me):
    t = me["t"]
    ids = segs_of(s, t)
    ahead = jnp.where(t > 0, segs_of(s, (t + 7) % PARTS), -1.0)
    later = jnp.where(t < PARTS - 1, segs_of(s, (t + 1) % PARTS), -1.0)
    lane = lax.broadcasted_iota(jnp.int32, (8, ROWS), 1)
    ids8, ahead8, later8 = (jnp.broadcast_to(v, (8, ROWS)) for v in (ids, ahead, later))
    one, zero = jnp.ones((8, ROWS), F32), jnp.zeros((8, ROWS), F32)
    row = lax.broadcasted_iota(jnp.int32, (8, ROWS), 0)
    top, low = zero, zero
    for k in (1, 2, 3):
        shifted = jnp.where(lane < k, pltpu.roll(ahead8, k, 1), pltpu.roll(ids8, k, 1))
        top = jnp.where((row == SAME + k) & (shifted == ids8), one, top)
        shifted = jnp.where(lane >= ROWS - k, pltpu.roll(later8, ROWS - k, 1), pltpu.roll(ids8, ROWS - k, 1))
        top = jnp.where((row == AFTER + k) & (shifted == ids8), one, top)
    last, before = ids8[:, ROWS - 1 :], ahead8[:, ROWS - 1 :]
    top = jnp.where((row == ENDING) & (ids8 == last), one, top)
    low = jnp.where((row == JOINED - 8) & (ids8 == before), one, low)
    low = jnp.where((row == KEPT - 8) & (last == before), one, low)
    low = jnp.where(row == IDS - 8, ids8, low)
    s.masks[...] = jnp.concatenate([top, low, jnp.zeros((112, ROWS), F32)], axis=0).T


def conv_sum(before, taps, bias, masks):
    total = bias + taps[3:4] * before[HALO:]
    for k in (1, 2, 3):
        shifted = before[HALO - k : HALO - k + ROWS]
        total = total + taps[3 - k : 4 - k] * (masks[:, SAME + k : SAME + k + 1] * shifted)
    return total


def enter_shared(s):
    before = dot(s.normed[...], s.w_shared[...], 1, 0)
    s.spre[...] = before
    total = conv_sum(before, s.conv_shared[...], s.bias_shared[...].reshape(1, 2 * STATE), s.masks[...])
    s.ssum[...] = total
    s.bc[...] = (total * jax.nn.sigmoid(total)).astype(BF16)


def enter_value(s, t):
    cols = of_part(t)
    block = s.prm[t]
    before = dot(s.normed[...], weights_of(s.wv, t)[:, :WIDE], 1, 0)
    s.vpre[:, cols] = before
    total = conv_sum(before, block[0:4, :WIDE], block[4:5, :WIDE], s.masks[...])
    s.vsum[:, cols] = total
    s.vals[:, cols] = (total * jax.nn.sigmoid(total)).astype(BF16)


def step_weights(s):
    total = weights_of(s.wv, 0)[:, 128:]
    for t in range(1, PARTS):
        total = total + weights_of(s.wv, t)[:, 128:]
    return total


def enter_step(s):
    heads = s.prm[0, 6:8]
    for t in range(1, PARTS):
        heads = heads + s.prm[t, 6:8]
    is_head = lax.broadcasted_iota(jnp.int32, (ROWS, 128), 1) < HEADS
    s.rate[...] = jnp.where(is_head[0:8], -jnp.exp(jnp.broadcast_to(heads[0:1, 128:], (8, 128))), 0.0)
    s.skip[...] = jnp.broadcast_to(heads[1:2, :128], (8, 128))
    s.wstep[...] = step_weights(s)
    step = dot(s.normed[HALO:], s.wstep[...], 1, 0)
    raw = jnp.where(is_head, pltpu.roll(step, 64, 1) + heads[0:1, :128], 0.0)
    s.raw[...] = raw
    dt = jnp.where(is_head, jnp.maximum(raw, 0.0) + jnp.log1p(jnp.exp(-jnp.abs(raw))), 0.0)
    s.dt[...] = dt
    logs = dot(lower_triangle().astype(F32), dt * s.rate[0:1], 1, 0, HIGHEST)
    s.logs[...] = logs
    s.dt_t[...] = dt.T
    s.logs_t[...] = logs.T


def make_fresh(s):
    logs, masks = s.logs[...], s.masks[...]
    last = logs[ROWS - 1 :]
    top, rest = halves(masks[:, ENDING : ENDING + 1] * jnp.exp(last - logs) * s.dt[...])
    s.weight_top[...] = top
    s.weight_rest[...] = rest

    def body(cols):
        weights = dot(s.weight_top[...], s.lanes[:, cols], 1, 0) + dot(s.weight_rest[...], s.lanes[:, cols], 1, 0)
        weighted = (s.vals[:, cols].astype(F32) * weights).astype(BF16)
        s.state[:, cols] = dot(s.bc[:, :STATE], weighted, 0, 0).astype(BF16)

    columns(body)
    kept = masks[0:8, KEPT : KEPT + 1] * jnp.exp(jnp.broadcast_to(last, (8, 128)))
    top, rest = halves(to_units(kept, s.lanes[...])[0:1])
    top, rest = top.astype(F32), rest.astype(F32)
    pack(s.fresh, s.state)
    row = lax.broadcasted_iota(jnp.int32, (16, 128), 0)
    for k in range(PARTS):
        tail = jnp.zeros((16, 128), F32)
        for at, part, tile in ((0, top, k), (1, rest, k), (2, top, 8 + k // 2), (3, rest, 8 + k // 2)):
            tail = jnp.where(row == at, part[:, tile * 128 : tile * 128 + 128], tail)
        s.fresh[k, STATE + 64 :] = tail.astype(BF16)


def scan_states(s):
    state = jnp.zeros((STATE + 64, 128), F32)
    for b in range(PARTS):
        s.state_out[b] = state.astype(BF16)
        state = s.fresh_in[b, : STATE + 64].astype(F32) + kept_of(s, b) * state


def scan_back(s):
    coming = jnp.zeros((STATE + 64, 128), F32)
    for b in reversed(range(PARTS)):
        s.coming_out[b] = coming.astype(BF16)
        coming = s.dstate_in[b].astype(F32) + kept_of(s, b) * coming


def tiles(low, high, body, width=128):
    def step(tile, carry):
        body(tile, pl.ds(pl.multiple_of(tile * width, width), width))
        return carry

    lax.fori_loop(low, high, step, 0, unroll=6 if width == 256 else 2)


def columns(body):
    tiles(0, INNER // 256, lambda tile, cols: body(cols), 256)


def make_scores(s):
    masks = s.masks[...]
    ids_row = masks.T[IDS : IDS + 1]
    allowed = lower_triangle() & (masks[:, IDS : IDS + 1] == ids_row)
    s.allowed[...] = jnp.where(allowed, 1.0, 0.0)
    s.scores[...] = jnp.where(allowed, dot(s.bc[:, STATE:], s.bc[:, :STATE], 1, 1), 0.0)


def mix_inside(s, low, high):
    def body(tile, cols):
        logs = pltpu.roll(s.logs[...], (128 - 2 * tile) % 128, 1)
        total = jnp.zeros((ROWS, 128), F32)
        for j, vals in enumerate(pair(s.vals, cols, first_half())):
            h = 2 * tile + j
            gaps = jnp.minimum(logs[:, j : j + 1] - s.logs_t[pl.ds(h, 1), :], 0.0)
            decay = (jnp.exp(gaps) * s.dt_t[pl.ds(h, 1), :]).astype(BF16)
            s.dec[h] = decay
            mix = (s.scores[...] * decay.astype(F32)).astype(BF16)
            total = total + dot(mix, vals, 1, 0)
        s.inner[:, cols] = total

    tiles(low, high, body)


def add_states(s):
    top, rest = halves(s.masks[:, JOINED : JOINED + 1] * jnp.exp(s.logs[...]))
    s.weight_top2[...] = top
    s.weight_rest2[...] = rest
    unpack(s.state, s.state_in)
    s.skips[...] = to_units(s.skip[...], s.lanes[...])
    s.squares[...] = jnp.zeros_like(s.squares)

    def body(cols):
        carried = dot(s.weight_top2[...], s.lanes[:, cols], 1, 0) + dot(s.weight_rest2[...], s.lanes[:, cols], 1, 0)
        inner = s.inner[:, cols] + dot(s.bc[:, STATE:], s.state[:, cols], 1, 0) * carried
        s.inner[:, cols] = inner
        gate = s.gate[:, cols]
        gated = (inner + s.skips[0:1, cols] * s.vals[:, cols].astype(F32)) * (gate * jax.nn.sigmoid(gate))
        s.normal[:, cols] = gated
        s.squares[...] = s.squares[...] + gated * gated

    columns(body)


def gated_norm(s):
    inverse = lax.rsqrt(jnp.sum(s.squares[...], axis=1, keepdims=True) / INNER + EPSILON)
    s.inverse[...] = jnp.broadcast_to(inverse, (ROWS, 128))
    for t in range(PARTS):
        s.gain_out[:, of_part(t)] = jnp.broadcast_to(s.prm[t, 5:6, :WIDE], (8, WIDE))
    s.squares[...] = jnp.zeros_like(s.squares)

    def body(cols):
        normal = s.normal[:, cols] * s.inverse[:, 0:1]
        s.normal[:, cols] = normal
        gain = s.gain_out[0:1, cols]
        s.nout[:, cols] = (normal * gain).astype(BF16)
        d_out = s.dout[:, cols]
        product = d_out * normal
        s.small[5:6, cols] = jnp.sum(product, axis=0, keepdims=True)
        s.squares[...] = s.squares[...] + product * gain

    columns(body)


def project_back(s, t):
    cols = of_part(t)
    s.dout[:, cols] = dot(s.cot[...], weights_of(s.wg, t)[:, WIDE:], 1, 0)


def project_out(s):
    branch = s.x[...].astype(F32)
    for t in range(PARTS):
        branch = branch + dot(s.nout[:, of_part(t)], weights_of(s.wg, t)[:, WIDE:], 1, 1)
    s.result_in[...] = branch.astype(BF16)


def gated_norm_back(s):
    total = jnp.sum(s.squares[...], axis=1, keepdims=True) / INNER
    s.dots[...] = jnp.broadcast_to(total, (ROWS, 128))

    def body(cols):
        d_scaled = s.dout[:, cols] * s.gain_out[0:1, cols]
        d_gated = s.inverse[:, 0:1] * (d_scaled - s.normal[:, cols] * s.dots[:, 0:1])
        gate = s.gate[:, cols]
        sig = jax.nn.sigmoid(gate)
        vals = s.vals[:, cols].astype(F32)
        mixed = s.inner[:, cols] + s.skips[0:1, cols] * vals
        d_mixed = d_gated * (gate * sig)
        s.dgate[:, cols] = (d_gated * mixed * sig * (1.0 + gate * (1.0 - sig))).astype(BF16)
        s.small[6:7, cols] = jnp.sum(d_mixed * vals, axis=0, keepdims=True)
        s.dy[:, cols] = d_mixed.astype(BF16)
        s.dval[:, cols] = s.skips[0:1, cols] * d_mixed
        lanes = s.lanes[:, cols]
        carried = dot(s.weight_top2[...], lanes, 1, 0) + dot(s.weight_rest2[...], lanes, 1, 0)
        d_carried = (d_mixed * carried).astype(BF16)
        s.dcar[:, cols] = d_carried
        s.dfresh[:, cols] = dot(s.bc[:, STATE:], d_carried, 0, 0).astype(BF16)

    columns(body)


def states_back(s):
    pack(s.dstate, s.dfresh)


def mix_back(s, low, high):
    def body(tile, cols):
        total = jnp.zeros((ROWS, 128), F32)
        d_scores = s.dscores[...]
        first = first_half()
        for j, (vals, grads) in enumerate(zip(pair(s.vals, cols, first), pair(s.dy, cols, first))):
            h = 2 * tile + j
            d_mix = dot(grads, vals, 1, 1)
            decay = s.dec[h].astype(F32)
            d_scores = d_scores + d_mix * decay
            total = total + dot((s.scores[...] * decay).astype(BF16), grads, 0, 0)
        s.dscores[...] = d_scores
        s.dval[:, cols] = s.dval[:, cols] + total
        s.dout[:, cols] = total * s.vals[:, cols].astype(F32)

    tiles(low, high, body)


def after_mix_back(s):
    s.direct[...] = jnp.zeros_like(s.direct)
    s.dlog[...] = jnp.zeros_like(s.dlog)

    def body(cols):
        lanes = s.lanes[:, cols]
        from_values = s.dout[:, cols]
        s.direct[...] = s.direct[...] + to_heads(from_values, lanes)
        s.dlog[...] = s.dlog[...] + to_heads(s.dy[:, cols].astype(F32) * s.inner[:, cols] - from_values, lanes)

    columns(body)
    d_scores = (s.dscores[...] * s.allowed[...]).astype(BF16)
    s.dbc[:, :STATE] = dot(d_scores, s.bc[:, STATE:], 0, 0)
    s.dbc[:, STATE:] = dot(d_scores, s.bc[:, :STATE], 1, 0) + dot(s.dcar[...], s.state[...], 1, 1)


def leave(s):
    lanes = s.lanes[...]
    logs, dt, raw, masks = s.logs[...], s.dt[...], s.raw[...], s.masks[...]
    unpack(s.coming, s.coming_in)
    last = logs[ROWS - 1 :]
    s.through[...] = jnp.zeros_like(s.through)

    def body(cols):
        lanes = s.lanes[:, cols]
        weights = dot(s.weight_top[...], lanes, 1, 0) + dot(s.weight_rest[...], lanes, 1, 0)
        weighted = s.vals[:, cols].astype(F32) * weights
        below = dot(s.bc[:, :STATE], s.coming[:, cols], 1, 0)
        s.dsum[:ROWS, cols] = (s.dval[:, cols] + weights * below) * silu_slope(s.vsum[:, cols])
        s.through[...] = s.through[...] + to_heads(weighted * below, lanes)
        s.dbc[:, :STATE] = s.dbc[:, :STATE] + dot(weighted.astype(BF16), s.coming[:, cols], 1, 1)

    columns(body)
    through, coming = s.through[...], s.coming[...]
    kept = masks[0:8, KEPT : KEPT + 1] * jnp.exp(jnp.broadcast_to(last, (8, 128)))
    held = jnp.sum(coming.astype(F32) * s.state[...].astype(F32), axis=0, keepdims=True)
    d_kept = to_heads(jnp.broadcast_to(held, (8, INNER)), lanes)
    d_last = jnp.sum(through, axis=0, keepdims=True) + (d_kept * kept)[0:1]
    row = lax.broadcasted_iota(jnp.int32, (ROWS, ROWS), 0)
    upper = row <= lax.broadcasted_iota(jnp.int32, (ROWS, ROWS), 1)
    d_rate = dot(upper.astype(F32), s.dlog[...] - through, 1, 0, HIGHEST) + d_last
    by_rate = dt * s.rate[0:1] * d_rate
    slope = jnp.where(raw < -15.0, 1.0, jax.nn.sigmoid(raw) / jnp.where(raw < -15.0, 1.0, dt))
    is_head = lax.broadcasted_iota(jnp.int32, (ROWS, 128), 1) < HEADS
    d_step = jnp.where(is_head, (s.direct[...] + through + by_rate) * slope, 0.0)
    s.dstep[...] = d_step.astype(BF16)
    s.small[7:8, 0:128] = jnp.sum(d_step, axis=0, keepdims=True)
    s.small[7:8, 128:256] = jnp.sum(by_rate, axis=0, keepdims=True)
    s.dsum[:ROWS, INNER:] = s.dbc[...] * silu_slope(s.ssum[...])
    s.edge[...] = s.dsum[0:8]


def conv_grads(s):
    masks = s.masks[...]

    def rows_of(d_sum, before_ref, cols):
        rows = []
        for k in (3, 2, 1):
            shifted = masks[:, SAME + k : SAME + k + 1] * before_ref[HALO - k : HALO - k + ROWS, cols]
            rows.append(jnp.sum(d_sum * shifted, axis=0, keepdims=True))
        rows.append(jnp.sum(d_sum * before_ref[HALO:, cols], axis=0, keepdims=True))
        rows.append(jnp.sum(d_sum, axis=0, keepdims=True))
        return rows

    def body(cols):
        for k, row in enumerate(rows_of(s.dsum[:ROWS, cols], s.vpre, cols)):
            s.small[k : k + 1, cols] = row

    columns(body)
    for k, row in enumerate(rows_of(s.dsum[:ROWS, INNER:], s.spre, EVERY)):
        s.small[7:8, 256 * (k + 1) : 256 * (k + 2)] = row


def conv_back(s):
    masks = s.masks[...]

    def back(cols, taps):
        total = taps[3:4] * s.dsum[:ROWS, cols]
        for k in (1, 2, 3):
            ahead = masks[:, AFTER + k : AFTER + k + 1] * s.dsum[k : k + ROWS, cols]
            total = total + taps[3 - k : 4 - k] * ahead
        return total.astype(BF16)

    for t in range(PARTS):
        cols = of_part(t)
        s.dvlow[:, cols] = back(cols, s.prm[t, 0:4, :WIDE])
    s.dshared[...] = back(slice(INNER, INNER + 2 * STATE), s.conv_shared[...])


def as_block(v):
    return v.reshape(4, 2, 2, 3, 16, v.shape[-1])


def parts_g(s, t):
    cols = of_part(t)
    gates = dot(s.normed_t[...], s.dgate[:, cols], 1, 0)
    outs = dot(s.cot_t[...], s.nout[:, cols], 1, 0)
    s.pg[t // 4, t % 4] = as_block(jnp.concatenate([gates, outs], axis=1).astype(BF16))


def parts_shared(s):
    shared = dot(s.normed_t[...], s.dshared[...], 1, 0)
    blank = jnp.zeros((4, 128), F32)
    for k in range(128):
        strip = shared[k // 2 * 12 : k // 2 * 12 + 12, k % 2 * 128 : k % 2 * 128 + 128]
        s.ps[k // 32, k // 16 % 2, k // 8 % 2, k % 8] = jnp.concatenate([strip, blank], axis=0).astype(BF16)


def parts_v(s):
    steps = dot(s.normed_t[...], s.dstep[...], 1, 0)[:, :64].astype(BF16)
    for t in range(PARTS):
        values = dot(s.normed_t[...], s.dvlow[:, of_part(t)], 1, 0).astype(BF16)
        s.pv[t // 4, t % 4] = as_block(jnp.concatenate([values, steps], axis=1))


def normed_back_g(s):
    total = jnp.zeros((ROWS, D), F32)
    for t in range(PARTS):
        total = total + dot(s.dgate[:, of_part(t)], weights_of(s.wg, t)[:, :WIDE], 1, 1)
    s.dnormed[...] = total


def normed_back_v(s):
    total = s.dnormed[...] + dot(s.dshared[...], s.w_shared[...], 1, 1)
    total = total + dot(pltpu.roll(s.dstep[...].astype(F32), 64, 1).astype(BF16), s.wstep[...], 1, 1)
    for t in range(PARTS):
        total = total + dot(s.dvlow[:, of_part(t)], weights_of(s.wv, t)[:, :WIDE], 1, 1)
    x = s.x[...].astype(F32)
    inverse = lax.rsqrt(jnp.mean(x * x, axis=1, keepdims=True) + EPSILON)
    scaled = x * inverse
    d_in = total * s.in_gain[...].reshape(1, D)
    gains = jnp.sum(total * scaled, axis=0, keepdims=True)
    s.gain_row[...] = jnp.zeros_like(s.gain_row)
    for k in range(D // 128):
        s.gain_row[k : k + 1] = gains[:, k * 128 : k * 128 + 128]
    centred = jnp.mean(d_in * scaled, axis=1, keepdims=True)
    s.resid_in[...] = inverse * (d_in - scaled * centred) + s.cot[...].astype(F32)


def own_part(row, me, width):
    total = jnp.where(me["t"] == 0, row[:, :width], 0.0)
    for t in range(1, PARTS):
        total = total + jnp.where(me["t"] == t, row[:, t * width : (t + 1) * width], 0.0)
    return total


def closing_kernel(*refs):
    names = [*RESULTS, *OUTPUTS]
    s = types.SimpleNamespace(**dict(zip(names, refs)))
    me = place()
    s.result[...] = s.result_in[...]
    s.grad_resid[...] = s.resid_in[...]
    s.grad_w_value[...] = s.block_v[:, :WIDE]
    steps = s.block_v[:, 128:].T
    s.grad_w_step[...] = sum(jnp.where(me["t"] == t, steps[64 + 3 * t : 67 + 3 * t], 0.0) for t in range(PARTS))
    s.grad_w_gate[...] = s.block_g[:, :WIDE]
    s.grad_w_out[...] = s.block_g[:, WIDE:]
    total = s.total[...]
    own = own_part(total, me, WIDE)
    s.grad_conv_inner[...] = own[0:4]
    s.grad_bias_inner[...] = own[4:5].reshape(WIDE)
    s.grad_out_gain[...] = own[5:6].reshape(WIDE)
    for k in range(4):
        s.grad_conv_shared[k : k + 1] = total[7:8, 256 * (k + 1) : 256 * (k + 2)]
    s.grad_bias_shared[...] = total[7:8, 1280:].reshape(2 * STATE)
    s.grad_step_bias[...] = own_part(total[7:8, 0:24], me, 3)
    s.grad_decay_log[...] = own_part(total[7:8, 128:152], me, 3)
    s.grad_skip_gain[...] = own_part(to_heads(total, head_lanes())[6:7, 0:24], me, 3)
    for k in range(D // 128):
        s.grad_in_gain[k * 128 : k * 128 + 128] = s.gains[k]
    for k in range(128):
        tile = s.tails_in[k // 32, k // 16 % 2, k // 8 % 2, k % 8].astype(F32)
        s.grad_w_shared[k // 2 * 12 : k // 2 * 12 + 12, k % 2 * 128 : k % 2 * 128 + 128] = tile[:12]


INPUTS = dict(
    x=0, cot=0, segs=0, in_gain=0, w_gate=0, w_value=0, w_step=0, w_shared=0, conv_inner=0, bias_inner=0,
    conv_shared=0, bias_shared=0, step_bias=1, decay_log=1, skip_gain=1, out_gain=0, w_out=0,
)
OUTPUTS = dict(
    result=((ROWS, D), BF16), grad_resid=((ROWS, D), F32), grad_in_gain=((D,), F32),
    grad_w_gate=((48, WIDE), F32), grad_w_value=((48, WIDE), F32), grad_w_step=((3, 48), F32),
    grad_w_shared=((D, 2 * STATE), F32), grad_conv_inner=((4, WIDE), F32), grad_bias_inner=((WIDE,), F32),
    grad_conv_shared=((4, 2 * STATE), F32), grad_bias_shared=((2 * STATE,), F32),
    grad_step_bias=((1, 3), F32), grad_decay_log=((1, 3), F32), grad_skip_gain=((1, 3), F32),
    grad_out_gain=((WIDE,), F32), grad_w_out=((48, WIDE), F32),
)
RESULTS = dict(
    result_in=((ROWS, D), BF16), resid_in=((ROWS, D), F32), block_v=((48, PACK_V), F32),
    block_g=((48, PACK_G), F32), total=((8, INNER), F32), gains=((8, 128), F32),
    tails_in=((4, 2, 2, 8, 16, 128), BF16),
)
TORUS = (2, 4, 4, 2, 2, 3, 16)


def reduce_scratch(width, relayed, orders):
    block = (16, width)
    last = [free_shape(order[2:]) + block for order in orders]
    half = [free_shape(order[2:], True) + block for order in orders]
    line = [free_shape(order[1:]) + block for order in orders]
    kinds = [(4, last), (2 if relayed else 3, last), (3, line)]
    shapes = [(lead,) + shape for lead, shapes in kinds for shape in shapes] + [(3, 3) + block]
    return shapes + ([(2,) + shape for shape in half] if relayed else [])


SCRATCH = dict(
    wv=(TORUS + (PACK_V,), BF16), wg=(TORUS + (PACK_G,), BF16),
    pv=(TORUS + (PACK_V,), BF16), pg=(TORUS + (PACK_G,), BF16), ps=((4, 2, 2, 8, 16, 128), BF16), heard_s=((4, 2, 8, 16, 128), BF16),
    got_s=((64, 16, 128), BF16),
    own_v=((3, 16, PACK_V), BF16), own_g=((3, 16, PACK_G), BF16), own_t=((16, 128), BF16), turned=((64, 128), F32),
    own_p=((8, 256), F32), prm=((PARTS, 8, 256), F32), ahead=((HALO, D), BF16),
    normed=((HALO + ROWS, D), BF16), normed_t=((D, ROWS), BF16), cot_t=((D, ROWS), BF16),
    masks=((ROWS, 128), F32), lanes=((128, INNER), BF16), dfresh=((STATE, INNER), BF16),
    weight_top=((ROWS, 128), BF16), weight_rest=((ROWS, 128), BF16), through=((ROWS, 128), F32),
    weight_top2=((ROWS, 128), BF16), weight_rest2=((ROWS, 128), BF16), dots=((ROWS, 128), F32),
    squares=((ROWS, 256), F32),
    vpre=((HALO + ROWS, INNER), F32), vsum=((ROWS, INNER), F32), vals=((ROWS, INNER), BF16),
    spre=((HALO + ROWS, 256), F32), ssum=((ROWS, 256), F32), bc=((ROWS, 256), BF16),
    rate=((8, 128), F32), skip=((8, 128), F32), skips=((8, INNER), F32), gain_out=((8, INNER), F32),
    wstep=((D, 128), BF16), raw=((ROWS, 128), F32), dt=((ROWS, 128), F32), logs=((ROWS, 128), F32),
    dt_t=((128, ROWS), F32), logs_t=((128, ROWS), F32),
    fresh=((PARTS, 208, 128), BF16), fresh_in=((PARTS, 208, 128), BF16),
    state_out=((PARTS, STATE + 64, 128), BF16), state_in=((PARTS, STATE + 64, 128), BF16),
    dstate=((PARTS, STATE + 64, 128), BF16), dstate_in=((PARTS, STATE + 64, 128), BF16),
    coming_out=((PARTS, STATE + 64, 128), BF16), coming_in=((PARTS, STATE + 64, 128), BF16),
    state=((STATE, INNER), BF16),
    scores=((ROWS, ROWS), F32), dscores=((ROWS, ROWS), F32), allowed=((ROWS, ROWS), F32),
    dec=((HEADS, ROWS, ROWS), BF16),
    inner=((ROWS, INNER), F32),
    gate=((ROWS, INNER), F32), normal=((ROWS, INNER), F32),
    inverse=((ROWS, 128), F32), nout=((ROWS, INNER), BF16), dout=((ROWS, INNER), F32),
    dgate=((ROWS, INNER), BF16), dy=((ROWS, INNER), BF16), dcar=((ROWS, INNER), BF16),
    direct=((ROWS, 128), F32), dlog=((ROWS, 128), F32),
    dbc=((ROWS, 256), F32), dstep=((ROWS, 128), BF16),
    dsum=((ROWS + 8, INNER + 256), F32), edge=((8, INNER + 256), F32),
    dshared=((ROWS, 256), BF16),
    small=((8, INNER), F32), small_sums=((4, 8, INNER), F32), small_got=((10, 8, INNER), F32),
    gain_row=((8, 128), F32), gain_sums=((4, 8, 128), F32), gain_got=((10, 8, 128), F32),
)
SEMAPHORES = dict(
    gather_v=45, gather_g=45, shared=4, reduce_g=42, reduce_v=42,
    total=10, total_gain=10, swap_p=8, swap1=8, swap2=8, swap3=8, swap4=8, edges=2,
)


def reducer(me, orders, parts, refs, sems):
    return Reduce(me, orders, parts, refs[0:3], refs[10:13] or None, refs[3:6], refs[6:9], refs[9], sems)


REDUCE_G = reduce_scratch(PACK_G, True, ASIDE)
REDUCE_V = reduce_scratch(PACK_V, False, ORDERS)


def everything(s, sems):
    me = place()
    dp, t = me["dp"], me["t"]
    after, before = (dp, (t + 1) % PARTS), (dp, (t + 7) % PARTS)
    greet(me)
    make_blocks(s, me)
    in_gain = s.in_gain[...].reshape(1, D)
    s.normed[HALO:] = norm_of(s.x[...], in_gain)
    make_masks(s, me)
    greeted()

    gather_v = Gather(me, s.own_v, s.wv, sems.gather_v, False)
    gather_g = Gather(me, s.own_g, s.wg, sems.gather_g, True)
    gather_v.first()
    halo = transfer(s.x.at[pl.ds(ROWS - HALO, HALO)], s.ahead, sems.edges, 0, after)
    gather_g.first()
    params = [transfer(s.own_p, s.prm.at[t], sems.swap_p, by, (dp, (t + by) % PARTS)) for by in range(1, PARTS)]
    s.prm[t] = s.own_p[...]
    s.lanes[...] = head_lanes()
    gather_v.second()
    halo.wait_recv()
    s.normed[:HALO] = norm_of(s.ahead[...], in_gain)
    gather_v.third()
    gather_g.second()
    enter_shared(s)
    make_scores(s)
    s.normed_t[...] = s.normed[HALO:].T
    s.cot_t[...] = s.cot[...].T
    for copy in params:
        copy.wait_recv()
    gather_v.relay()
    gather_v.finish()
    gather_g.third()
    gather_v.settle()

    enter_step(s)
    for part in range(PARTS):
        enter_value(s, part)
    make_fresh(s)
    swap1 = Swap(me, s.fresh, s.fresh_in, sems.swap1)
    swap1.start()
    gather_g.relay()
    mix_inside(s, 0, 8)
    swap1.wait()
    scan_states(s)
    swap2 = Swap(me, s.state_out, s.state_in, sems.swap2)
    swap2.start()
    gather_g.finish()
    mix_inside(s, 8, 12)
    gather_g.settle()
    for part in range(PARTS):
        s.gate[:, of_part(part)] = dot(s.normed[HALO:], weights_of(s.wg, part)[:, :WIDE], 1, 0)
        project_back(s, part)
    swap2.wait()
    add_states(s)
    gated_norm(s)
    gated_norm_back(s)
    states_back(s)
    swap3 = Swap(me, s.dstate, s.dstate_in, sems.swap3)
    swap3.start()
    for part in range(PARTS):
        parts_g(s, part)
    reduce_g = reducer(me, ASIDE, s.pg, s.refs_g, sems.reduce_g)
    reduce_g.swap()
    s.dscores[...] = jnp.zeros_like(s.dscores)
    project_out(s)
    mix_back(s, 0, 2)
    reduce_g.relay()
    mix_back(s, 2, 6)
    swap3.wait()
    scan_back(s)
    swap4 = Swap(me, s.coming_out, s.coming_in, sems.swap4)
    swap4.start()
    mix_back(s, 6, 8)
    reduce_g.third()
    mix_back(s, 8, 12)
    after_mix_back(s)
    normed_back_g(s)
    swap4.wait()
    leave(s)
    edge = transfer(s.edge, s.dsum.at[pl.ds(ROWS, 8)], sems.edges, 1, before)
    conv_grads(s)
    total = Total(me, s.small, s.small_sums, s.small_got, sems.total)
    total.along(0)
    reduce_g.second()
    edge.wait_recv()
    conv_back(s)
    parts_shared(s)
    shared = Shared(me, s.ps, s.heard_s, s.got_s, s.own_t, s.tails_in, sems.shared)
    shared.swap()
    parts_v(s)
    reduce_v = reducer(me, ORDERS, s.pv, s.refs_v, sems.reduce_v)
    reduce_v.swap()
    shared.scatter()
    reduce_v.relay()
    reduce_v.third()
    total.add(0)
    total.along(1)
    normed_back_v(s)
    gain = Total(me, s.gain_row, s.gain_sums, s.gain_got, sems.total_gain)
    gain.along(0)
    reduce_g.first()
    shared.gather()
    gain.add(0)
    gain.along(1)
    reduce_v.second()
    total.add(1)
    total.along(2)
    gain.add(1)
    gain.along(2)
    reduce_v.first()
    total.add(2)
    total.along(3)
    gain.add(2)
    gain.along(3)
    shared.share()
    for p in range(3):
        s.block_g[16 * p : 16 * p + 16] = reduce_g.result(p)
    for p in range(3):
        s.block_v[16 * p : 16 * p + 16] = reduce_v.result(p)
    total.add(3)
    s.total[...] = s.small_sums[3]
    gain.add(3)
    s.gains[...] = s.gain_sums[3]
    shared.finish()

    for channel in (gather_v, gather_g, shared, reduce_g, reduce_v, total, gain, swap1, swap2, swap3, swap4):
        channel.drain()
    for copy in [halo, edge, *params]:
        copy.wait_send()


def kernel(*refs):
    tables = (INPUTS, RESULTS, SCRATCH)
    names = [name for table in tables for name in table]
    s = types.SimpleNamespace(**dict(zip(names, refs)))
    s.dval, s.dvlow = s.normal, s.dy
    s.dnormed, s.coming = s.gate.at[:, :D], s.dcar.at[:STATE]
    at = len(names)
    s.refs_g, at = refs[at : at + len(REDUCE_G)], at + len(REDUCE_G)
    s.refs_v, at = refs[at : at + len(REDUCE_V)], at + len(REDUCE_V)
    pairs = zip(refs[at::2], refs[at + 1 :: 2])
    everything(s, types.SimpleNamespace(**dict(zip(SEMAPHORES, pairs))))


def shards(*args):
    args = list(args)
    args[6] = args[6].T
    vmem, smem = pl.BlockSpec(memory_space=pltpu.VMEM), pl.BlockSpec(memory_space=pltpu.SMEM)
    scratch = [pltpu.VMEM(shape, dtype) for shape, dtype in SCRATCH.values()]
    scratch += [pltpu.VMEM(shape, BF16) for shape in REDUCE_G + REDUCE_V]
    for count in SEMAPHORES.values():
        scratch += [pltpu.SemaphoreType.DMA((count,)), pltpu.SemaphoreType.DMA((count,))]
    shapes = lambda table: tuple(jax.ShapeDtypeStruct(shape, dtype) for shape, dtype in table.values())
    results = pl.pallas_call(
        kernel,
        out_shape=shapes(RESULTS),
        in_specs=[smem if scalar else vmem for scalar in INPUTS.values()],
        out_specs=tuple(vmem for _ in RESULTS),
        scratch_shapes=scratch,
        compiler_params=pltpu.CompilerParams(
            collective_id=0, has_side_effects=True, vmem_limit_bytes=VMEM_LIMIT
        ),
    )(*args)
    outs = pl.pallas_call(
        closing_kernel,
        out_shape=shapes(OUTPUTS),
        in_specs=[vmem for _ in RESULTS],
        out_specs=tuple(vmem for _ in OUTPUTS),
    )(*results)
    outs = [out.reshape(3) if out.shape == (1, 3) else out for out in outs]
    outs[5] = outs[5].T
    return tuple(outs)


def solution(mesh):
    rows, cols = P(("dp", "tensor"), None), P("dp", "tensor")
    head, whole = P("tensor"), P()
    in_specs = (
        rows, rows, P("dp"), whole, cols, cols, cols, whole, P(None, "tensor"), head,
        whole, whole, head, head, head, head, cols,
    )
    out_specs = (
        rows, rows, whole, cols, cols, cols, whole, P(None, "tensor"), head,
        whole, whole, head, head, head, head, cols,
    )
    return jax.shard_map(shards, mesh=mesh, in_specs=in_specs, out_specs=out_specs, check_vma=False)
```

```python
import types

import jax
import jax.numpy as jnp
from jax import lax
from jax.experimental import pallas as pl
from jax.experimental.pallas import tpu as pltpu
from jax.sharding import PartitionSpec as P

D = 768
HEADS = 24
HEADDIM = 64
STATE = 128
INNER = 1536
ROWS = 256
HALO = 16
PARTS = 8
WIDE = 192
PACK_V = 256
PACK_G = 384
EPSILON = 1e-05
VMEM_LIMIT = 62 * 1024 * 1024
MESH = pl.DeviceIdType.MESH
HIGHEST = lax.Precision.HIGHEST
F32 = jnp.float32
BF16 = jnp.bfloat16

ORDERS = (("x", "y", "z"), ("y", "z", "x"), ("z", "x", "y"))
DIMS = ("x", "y", "z")
ASIDE = (("x", "y", "z"), ("y", "x", "z"), ("z", "y", "x"))
EVERY = slice(None)


def over(a, n):
    return lax.div(a, jnp.int32(n))


def rest_of(a, n):
    return lax.rem(a, jnp.int32(n))


def place():
    dp, tensor = lax.axis_index("dp"), lax.axis_index("tensor")
    x = rest_of(over(dp, 2), 2) * 2 + over(tensor, 4)
    return {"x": x, "y": rest_of(tensor, 4), "z": over(dp, 4), "core": rest_of(dp, 2), "dp": dp, "t": tensor}


def device_of(at):
    return (at["z"] * 4 + over(at["x"], 2) * 2 + at["core"], rest_of(at["x"], 2) * 4 + at["y"])


def moved(me, dim, by):
    return {**me, dim: rest_of(me[dim] + by, 4)}


def sibling(me):
    return {**me, "core": 1 - me["core"]}


def region(fixed, half=None):
    x_lo, x_hi = (rest_of(fixed["x"], 2), over(fixed["x"], 2)) if "x" in fixed else (EVERY, EVERY)
    y, z = fixed.get("y", EVERY), fixed.get("z", EVERY)
    if half is not None:
        if "x" not in fixed:
            x_lo = pl.ds(half, 1)
        else:
            y = pl.ds(half * 2, 2)
    return (x_lo, y, z, x_hi)


def free_shape(fixed, half=False):
    sizes = [[dim, size] for dim, size in (("x", 2), ("y", 4), ("z", 4), ("x", 2)) if dim not in fixed]
    if half:
        sizes[0][1] //= 2
    return tuple(size for dim, size in sizes)


def transfer(src, dst, sems, slot, target):
    copy = pltpu.make_async_remote_copy(
        src_ref=src,
        dst_ref=dst,
        send_sem=sems[0].at[slot],
        recv_sem=sems[1].at[slot],
        device_id=target,
        device_id_type=MESH,
    )
    copy.start()
    return copy


def send(src, dst, sems, slot, target):
    return transfer(src, dst, sems, slot, device_of(target))


def peer(me, step):
    z_x = rest_of(me["z"] * 2 + over(me["x"], 2) + over(step, 8), 8)
    return (z_x * 2 + me["core"], rest_of(me["t"] + rest_of(step, 8), 8))


def each_peer(body):
    def step(i, carry):
        body(i)
        return carry

    lax.fori_loop(1, 64, step, 0)


def neighbours(me):
    along = [device_of(moved(me, dim, by)) for dim in DIMS for by in (1, 2, 3)]
    return along + [device_of(sibling(me))] + [(me["dp"], ((me["t"] + 4) % 8 // 4) * 4 + (me["y"] + by) % 4) for by in (1, 2, 3)]


def greet(me):
    for other in neighbours(me):
        pl.semaphore_signal(pltpu.get_barrier_semaphore(), inc=1, device_id=other, device_id_type=MESH)


def greeted():
    pl.semaphore_wait(pltpu.get_barrier_semaphore(), 13)


GATHER_SLOTS = 15
REDUCE_SLOTS = 14


class Gather:
    def __init__(self, me, own, buf, sems, relayed):
        self.me, self.own, self.buf, self.sems, self.relayed = me, own, buf, sems, relayed
        self.sent, self.got = [], {}

    def unit(self, p, stage, value, half=None):
        order = ORDERS[p]
        fixed = {dim: self.me[dim] for dim in order[stage + 1 :]}
        fixed[order[stage]] = value
        return self.buf.at[region(fixed, half) + (self.me["core"], p)]

    def go(self, name, p, slot, piece, target, source=None):
        copy = send(piece if source is None else source, piece, self.sems, p * GATHER_SLOTS + slot, target)
        self.sent.append(copy)
        self.got[name, p] = copy

    def first(self):
        me = self.me
        for p in range(3):
            dim = ORDERS[p][0]
            for by in (1, 3, 2):
                self.go(("a", by), p, by - 1, self.unit(p, 0, me[dim]), moved(me, dim, by), self.own.at[p])
        here = region({dim: me[dim] for dim in DIMS}) + (me["core"],)
        self.buf[here] = self.own[...]

    def second(self):
        me = self.me
        for p in range(3):
            for by in (1, 3, 2):
                self.got[("a", by), p].wait_recv()
            dim = ORDERS[p][1]
            for by in (1, 3, 2):
                self.go(("b", by), p, 2 + by, self.unit(p, 1, me[dim]), moved(me, dim, by))

    def third(self):
        me = self.me
        for p in range(3):
            for by in (1, 3, 2):
                self.got[("b", by), p].wait_recv()
            dim = ORDERS[p][2]
            unit = self.unit(p, 2, me[dim])
            self.go(("c", 1), p, 6, unit, moved(me, dim, 1))
            self.go(("c", 3), p, 7, unit, moved(me, dim, 3))
            if not self.relayed:
                self.go(("c", 2), p, 8, unit, moved(me, dim, 2))
        for p in range(3):
            self.across(p, 10, me[ORDERS[p][2]])

    def across(self, p, slot, value, half=None):
        self.go(("s", slot), p, slot, self.unit(p, 2, value, half), sibling(self.me))

    def relay(self):
        me = self.me
        for p in range(3):
            dim = ORDERS[p][2]
            for step, by, half in ((1, 1, 0), (3, 3, 1)):
                self.got[("c", by), p].wait_recv()
                value = rest_of(me[dim] + 4 - by, 4)
                if self.relayed:
                    self.go(("r", half), p, 8 + half, self.unit(p, 2, value, half), moved(me, dim, by))
                self.across(p, 11 + half, value)

    def finish(self):
        me = self.me
        for p in range(3):
            across = rest_of(me[ORDERS[p][2]] + 2, 4)
            if self.relayed:
                for half in (0, 1):
                    self.got[("r", half), p].wait_recv()
                    self.across(p, 13 + half, across, half)
            else:
                self.got[("c", 2), p].wait_recv()
                self.across(p, 13, across)

    def settle(self):
        for p in range(3):
            for slot in (10, 11, 12, 13, 14) if self.relayed else (10, 11, 12, 13):
                self.got[("s", slot), p].wait_recv()

    def drain(self):
        for copy in self.sent:
            copy.wait_send()
        self.sent = []


class Reduce:
    def __init__(self, me, orders, parts, heard, relayed, got_c, got_b, got_a, sems):
        self.me, self.orders, self.parts, self.sems = me, orders, parts, sems
        self.heard, self.relayed, self.got_c, self.got_b, self.got_a = heard, relayed, got_c, got_b, got_a
        self.sent, self.got = [], {}

    def unit(self, p, stage, by, half=None):
        order = self.orders[p]
        fixed = {dim: self.me[dim] for dim in order[stage + 1 :]}
        fixed[order[stage]] = rest_of(self.me[order[stage]] + by, 4)
        return region(fixed, half)

    def mine(self, p, stage, by, half=None):
        return self.unit(p, stage, by, half) + (self.me["core"], p)

    def go(self, name, p, slot, src, dst, target):
        copy = send(src, dst, self.sems, p * REDUCE_SLOTS + slot, target)
        self.sent.append(copy)
        self.got[name, p] = copy

    def swap(self):
        me = self.me
        for by in (2, 1, 3, 0):
            for p in range(3):
                src = self.parts.at[self.unit(p, 2, by) + (1 - me["core"], p)]
                self.go(("s", by), p, by, src, self.heard[p].at[by], sibling(me))

    def heard_add(self, by):
        for p in range(3):
            self.got[("s", by), p].wait_recv()
            at = self.mine(p, 2, by)
            self.parts[at] = self.parts[at] + self.heard[p][by]

    def relay(self):
        for by in (2, 1, 3):
            self.heard_add(by)
            for p in range(3):
                dim = self.orders[p][2]
                if self.relayed is None:
                    src, dst = self.parts.at[self.mine(p, 2, by)], self.got_c[p].at[by - 1]
                    self.go(("c", by), p, 3 + by, src, dst, moved(self.me, dim, by))
                elif by == 2:
                    for to, half in ((1, 0), (3, 1)):
                        src = self.parts.at[self.mine(p, 2, 2, half)]
                        self.go(("r", half), p, 4 + half, src, self.relayed[p].at[half], moved(self.me, dim, to))

    def third(self):
        for p in range(3):
            dim = self.orders[p][2]
            for by, half in ((1, 0), (3, 1)):
                if self.relayed is not None:
                    self.got[("r", half), p].wait_recv()
                    at = self.mine(p, 2, by, half)
                    self.parts[at] = self.parts[at] + self.relayed[p][half]
                    src = self.parts.at[self.mine(p, 2, by)]
                    self.go(("c", by), p, 6 + half, src, self.got_c[p].at[half], moved(self.me, dim, by))
        self.heard_add(0)

    def second(self):
        for p in range(3):
            for by in (1, 3) if self.relayed is not None else (1, 3, 2):
                self.got[("c", by), p].wait_recv()
            at, got = self.mine(p, 2, 0), self.got_c[p]
            summed = self.parts[at].astype(F32) + (got[0].astype(F32) + got[1].astype(F32))
            if self.relayed is None:
                summed = summed + got[2].astype(F32)
            self.parts[at] = summed.astype(BF16)
            dim = self.orders[p][1]
            for by in (1, 3, 2):
                self.go(("b", by), p, 7 + by, self.parts.at[self.mine(p, 1, by)], self.got_b[p].at[by - 1], moved(self.me, dim, by))

    def first(self):
        for p in range(3):
            for by in (1, 3, 2):
                self.got[("b", by), p].wait_recv()
            at, got = self.mine(p, 1, 0), self.got_b[p]
            self.parts[at] = (
                (self.parts[at].astype(F32) + got[0].astype(F32)) + (got[1].astype(F32) + got[2].astype(F32))
            ).astype(BF16)
            dim = self.orders[p][0]
            for by in (1, 3, 2):
                self.go(("a", by), p, 10 + by, self.parts.at[self.mine(p, 0, by)], self.got_a.at[p, by - 1], moved(self.me, dim, by))

    def result(self, p):
        for by in (1, 3, 2):
            self.got[("a", by), p].wait_recv()
        got = self.got_a
        return (self.parts[self.mine(p, 0, 0)].astype(F32) + got[p, 0].astype(F32)) + (
            got[p, 1].astype(F32) + got[p, 2].astype(F32)
        )

    def drain(self):
        for copy in self.sent:
            copy.wait_send()
        self.sent = []


class Total:
    def __init__(self, me, own, sums, got, sems):
        self.me, self.own, self.sums, self.got, self.sems = me, own, sums, got, sems
        self.sent = []

    def along(self, stage):
        me, src = self.me, self.own if stage == 0 else self.sums.at[stage - 1]
        if stage == 0:
            peers = [(9, sibling(me))]
        else:
            dim = DIMS[3 - stage]
            peers = [((stage - 1) * 3 + by - 1, moved(me, dim, by)) for by in (1, 3, 2)]
        self.now = [send(src, self.got.at[slot], self.sems, slot, peer) for slot, peer in peers]
        self.sent += self.now

    def add(self, stage):
        for copy in self.now:
            copy.wait_recv()
        got = self.got
        if stage == 0:
            self.sums[0] = self.own[...] + got[9]
        else:
            base = (stage - 1) * 3
            self.sums[stage] = (self.sums[stage - 1] + got[base]) + (got[base + 1] + got[base + 2])

    def drain(self):
        for copy in self.sent:
            copy.wait_send()
        self.sent = []


class Shared:
    def __init__(self, me, tiles, heard, got, own, tails, sems):
        self.me, self.tiles, self.heard, self.got, self.own, self.tails = me, tiles, heard, got, own, tails
        self.sems = sems
        self.sent = []

    def at(self, device):
        return (over(device[0], 4), rest_of(over(device[0], 2), 2), rest_of(device[0], 2), device[1])

    def here(self):
        return self.at((self.me["dp"], self.me["t"]))

    def half(self, core):
        return (EVERY, EVERY, core)

    def across(self, src, dst, slot):
        copy = send(src, dst, self.sems, slot, sibling(self.me))
        self.sent.append(copy)
        return copy

    def swap(self):
        self.swapped = self.across(self.tiles.at[self.half(1 - self.me["core"])], self.heard, 0)

    def everyone(self, src, dst, slot):
        def go(i):
            to = peer(self.me, i)
            pltpu.make_async_remote_copy(
                src_ref=src(to), dst_ref=dst, send_sem=self.sems[0].at[slot], recv_sem=self.sems[1].at[slot],
                device_id=to, device_id_type=MESH,
            ).start()

        each_peer(go)

    def wait(self, kind, slot):
        all_tiles = self.got.at[pl.ds(0, 63)]
        pltpu.make_async_copy(all_tiles, all_tiles, self.sems[kind].at[slot]).wait()

    def scatter(self):
        self.swapped.wait_recv()
        mine = self.half(self.me["core"])
        self.tiles[mine] = self.tiles[mine] + self.heard[...]
        z, x_hi, _, t = self.here()
        place = (z * 2 + x_hi) * 8 + t
        self.everyone(lambda to: self.tiles.at[self.at(to)], self.got.at[place], 1)
        self.got[place] = self.tiles[self.here()]

    def gather(self):
        self.wait(1, 1)
        total = jnp.sum(self.got[...].astype(F32), axis=0).astype(BF16)
        self.own[...] = total
        self.everyone(lambda to: self.own, self.tails.at[self.here()], 2)
        self.tails[self.here()] = total

    def share(self):
        self.wait(1, 2)
        mine = self.tails.at[self.half(self.me["core"])]
        self.shared = self.across(mine, mine, 3)

    def finish(self):
        self.shared.wait_recv()

    def drain(self):
        self.wait(0, 1)
        self.wait(0, 2)
        for copy in self.sent:
            copy.wait_send()


class Swap:
    def __init__(self, me, src, got, sems):
        self.me, self.src, self.got, self.sems = me, src, got, sems
        self.copies = []

    def start(self):
        dp, t = self.me["dp"], self.me["t"]
        for by in (4, 2, 6, 1, 7, 3, 5):
            to = rest_of(t + by, PARTS)
            self.copies.append(transfer(self.src.at[to], self.got.at[t], self.sems, by, (dp, to)))
        self.got[t] = self.src[t]

    def wait(self):
        for copy in self.copies:
            copy.wait_recv()

    def drain(self):
        for copy in self.copies:
            copy.wait_send()
        self.copies = []


def dot(a, b, over_a, over_b, precision=None):
    return lax.dot_general(
        a, b, (((over_a,), (over_b,)), ((), ())), precision=precision, preferred_element_type=F32
    )


def head_lanes():
    head = lax.broadcasted_iota(jnp.int32, (128, INNER), 0)
    unit = lax.broadcasted_iota(jnp.int32, (128, INNER), 1)
    low = head * HEADDIM
    return jnp.where((unit >= low) & (unit < low + HEADDIM), 1.0, 0.0).astype(BF16)


def halves(v):
    top = v.astype(BF16)
    return top, (v - top.astype(F32)).astype(BF16)


def to_units(v, lanes):
    top, rest = halves(v)
    return dot(top, lanes, 1, 0) + dot(rest, lanes, 1, 0)


def to_heads(v, lanes):
    top, rest = halves(v)
    return dot(top, lanes, 1, 1) + dot(rest, lanes, 1, 1)


def lower_triangle():
    row = lax.broadcasted_iota(jnp.int32, (ROWS, ROWS), 0)
    return row >= lax.broadcasted_iota(jnp.int32, (ROWS, ROWS), 1)


def first_half():
    return lax.broadcasted_iota(jnp.int32, (ROWS, 128), 1) < HEADDIM


def silu_slope(v):
    sig = jax.nn.sigmoid(v)
    return sig * (1.0 + v * (1.0 - sig))


def of_part(t):
    return slice(t * WIDE, (t + 1) * WIDE)


def weights_of(buf, t):
    block = buf[t // 4, t % 4]
    return block.reshape(D, block.shape[-1])


def pair(ref, cols, first):
    both = ref[:, cols]
    zero = jnp.zeros_like(both)
    return jnp.where(first, both, zero), jnp.where(first, zero, both)


def norm_of(x, gain):
    x = x.astype(F32)
    inverse = lax.rsqrt(jnp.mean(x * x, axis=1, keepdims=True) + EPSILON)
    return (x * inverse * gain).astype(BF16)


def pack(buf, whole):
    for k in range(PARTS):
        other, low = 8 + k // 2, k % 2 * 64
        buf[k, :STATE] = whole[:, k * 128 : k * 128 + 128]
        buf[k, STATE : STATE + 64] = whole[low : low + 64, other * 128 : other * 128 + 128]


def unpack(whole, buf):
    for k in range(PARTS):
        other, low = 8 + k // 2, k % 2 * 64
        whole[:, k * 128 : k * 128 + 128] = buf[k, :STATE]
        whole[low : low + 64, other * 128 : other * 128 + 128] = buf[k, STATE : STATE + 64]


def kept_of(s, block):
    rows = s.fresh_in[block, STATE + 64 :].astype(F32)
    first = lax.broadcasted_iota(jnp.int32, (STATE + 64, 128), 0) < STATE
    return jnp.where(first, rows[0:1] + rows[1:2], rows[2:3] + rows[3:4])


def make_blocks(s, me):
    t = me["t"]
    row = lax.broadcasted_iota(jnp.int32, (64, 48), 0)
    given = s.w_step[...].astype(F32)
    steps = jnp.zeros((64, 48), F32)
    for k in range(3):
        steps = jnp.where(row == 3 * t + k, given[k : k + 1], steps)
    s.turned[...] = jnp.zeros_like(s.turned)
    s.turned[:, :48] = steps
    steps = s.turned[...].T[:48].astype(BF16)
    for p in range(3):
        rows = slice(16 * p, 16 * p + 16)
        s.own_v[p, :, :WIDE] = s.w_value[rows]
        s.own_v[p, :, WIDE:] = steps[rows]
        s.own_g[p, :, :WIDE] = s.w_gate[rows]
        s.own_g[p, :, WIDE:] = s.w_out[rows]
    lane = lax.broadcasted_iota(jnp.int32, (1, 256), 1)
    row6, row7 = jnp.zeros((1, 256), F32), jnp.zeros((1, 256), F32)
    for k in range(3):
        row6 = jnp.where(lane == 3 * t + k, s.step_bias[k], row6)
        row6 = jnp.where(lane == 128 + 3 * t + k, s.decay_log[k], row6)
        row7 = jnp.where(lane == 3 * t + k, s.skip_gain[k], row7)
    s.own_p[...] = jnp.zeros_like(s.own_p)
    s.own_p[0:4, :WIDE] = s.conv_inner[...]
    s.own_p[4:5, :WIDE] = s.bias_inner[...].reshape(1, WIDE)
    s.own_p[5:6, :WIDE] = s.out_gain[...].reshape(1, WIDE)
    s.own_p[6:7] = row6
    s.own_p[7:8] = row7


SAME, AFTER, ENDING, JOINED, KEPT, IDS = 0, 3, 7, 8, 9, 10


def segs_of(s, block):
    return s.segs[pl.ds(pl.multiple_of(block * ROWS, ROWS), ROWS)].reshape(1, ROWS).astype(F32)


def make_masks(s, me):
    t = me["t"]
    ids = segs_of(s, t)
    ahead = jnp.where(t > 0, segs_of(s, (t + 7) % PARTS), -1.0)
    later = jnp.where(t < PARTS - 1, segs_of(s, (t + 1) % PARTS), -1.0)
    lane = lax.broadcasted_iota(jnp.int32, (8, ROWS), 1)
    ids8, ahead8, later8 = (jnp.broadcast_to(v, (8, ROWS)) for v in (ids, ahead, later))
    one, zero = jnp.ones((8, ROWS), F32), jnp.zeros((8, ROWS), F32)
    row = lax.broadcasted_iota(jnp.int32, (8, ROWS), 0)
    top, low = zero, zero
    for k in (1, 2, 3):
        shifted = jnp.where(lane < k, pltpu.roll(ahead8, k, 1), pltpu.roll(ids8, k, 1))
        top = jnp.where((row == SAME + k) & (shifted == ids8), one, top)
        shifted = jnp.where(lane >= ROWS - k, pltpu.roll(later8, ROWS - k, 1), pltpu.roll(ids8, ROWS - k, 1))
        top = jnp.where((row == AFTER + k) & (shifted == ids8), one, top)
    last, before = ids8[:, ROWS - 1 :], ahead8[:, ROWS - 1 :]
    top = jnp.where((row == ENDING) & (ids8 == last), one, top)
    low = jnp.where((row == JOINED - 8) & (ids8 == before), one, low)
    low = jnp.where((row == KEPT - 8) & (last == before), one, low)
    low = jnp.where(row == IDS - 8, ids8, low)
    s.masks[...] = jnp.concatenate([top, low, jnp.zeros((112, ROWS), F32)], axis=0).T


def conv_sum(before, taps, bias, masks):
    total = bias + taps[3:4] * before[HALO:]
    for k in (1, 2, 3):
        shifted = before[HALO - k : HALO - k + ROWS]
        total = total + taps[3 - k : 4 - k] * (masks[:, SAME + k : SAME + k + 1] * shifted)
    return total


def enter_shared(s):
    before = dot(s.normed[...], s.w_shared[...], 1, 0)
    s.spre[...] = before
    total = conv_sum(before, s.conv_shared[...], s.bias_shared[...].reshape(1, 2 * STATE), s.masks[...])
    s.ssum[...] = total
    s.bc[...] = (total * jax.nn.sigmoid(total)).astype(BF16)


def enter_value(s, t):
    cols = of_part(t)
    block = s.prm[t]
    before = dot(s.normed[...], weights_of(s.wv, t)[:, :WIDE], 1, 0)
    s.vpre[:, cols] = before
    total = conv_sum(before, block[0:4, :WIDE], block[4:5, :WIDE], s.masks[...])
    s.vsum[:, cols] = total
    s.vals[:, cols] = (total * jax.nn.sigmoid(total)).astype(BF16)


def step_weights(s):
    total = weights_of(s.wv, 0)[:, 128:]
    for t in range(1, PARTS):
        total = total + weights_of(s.wv, t)[:, 128:]
    return total


def enter_step(s):
    heads = s.prm[0, 6:8]
    for t in range(1, PARTS):
        heads = heads + s.prm[t, 6:8]
    is_head = lax.broadcasted_iota(jnp.int32, (ROWS, 128), 1) < HEADS
    s.rate[...] = jnp.where(is_head[0:8], -jnp.exp(jnp.broadcast_to(heads[0:1, 128:], (8, 128))), 0.0)
    s.skip[...] = jnp.broadcast_to(heads[1:2, :128], (8, 128))
    s.wstep[...] = step_weights(s)
    step = dot(s.normed[HALO:], s.wstep[...], 1, 0)
    raw = jnp.where(is_head, pltpu.roll(step, 64, 1) + heads[0:1, :128], 0.0)
    s.raw[...] = raw
    dt = jnp.where(is_head, jnp.maximum(raw, 0.0) + jnp.log1p(jnp.exp(-jnp.abs(raw))), 0.0)
    s.dt[...] = dt
    logs = dot(lower_triangle().astype(F32), dt * s.rate[0:1], 1, 0, HIGHEST)
    s.logs[...] = logs
    s.dt_t[...] = dt.T
    s.logs_t[...] = logs.T


def make_fresh(s):
    logs, masks = s.logs[...], s.masks[...]
    last = logs[ROWS - 1 :]
    top, rest = halves(masks[:, ENDING : ENDING + 1] * jnp.exp(last - logs) * s.dt[...])
    s.weight_top[...] = top
    s.weight_rest[...] = rest

    def body(cols):
        weights = dot(s.weight_top[...], s.lanes[:, cols], 1, 0) + dot(s.weight_rest[...], s.lanes[:, cols], 1, 0)
        weighted = (s.vals[:, cols].astype(F32) * weights).astype(BF16)
        s.state[:, cols] = dot(s.bc[:, :STATE], weighted, 0, 0).astype(BF16)

    columns(body)
    kept = masks[0:8, KEPT : KEPT + 1] * jnp.exp(jnp.broadcast_to(last, (8, 128)))
    top, rest = halves(to_units(kept, s.lanes[...])[0:1])
    top, rest = top.astype(F32), rest.astype(F32)
    pack(s.fresh, s.state)
    row = lax.broadcasted_iota(jnp.int32, (16, 128), 0)
    for k in range(PARTS):
        tail = jnp.zeros((16, 128), F32)
        for at, part, tile in ((0, top, k), (1, rest, k), (2, top, 8 + k // 2), (3, rest, 8 + k // 2)):
            tail = jnp.where(row == at, part[:, tile * 128 : tile * 128 + 128], tail)
        s.fresh[k, STATE + 64 :] = tail.astype(BF16)


def scan_states(s):
    state = jnp.zeros((STATE + 64, 128), F32)
    for b in range(PARTS):
        s.state_out[b] = state.astype(BF16)
        state = s.fresh_in[b, : STATE + 64].astype(F32) + kept_of(s, b) * state


def scan_back(s):
    coming = jnp.zeros((STATE + 64, 128), F32)
    for b in reversed(range(PARTS)):
        s.coming_out[b] = coming.astype(BF16)
        coming = s.dstate_in[b].astype(F32) + kept_of(s, b) * coming


def tiles(low, high, body, width=128):
    def step(tile, carry):
        body(tile, pl.ds(pl.multiple_of(tile * width, width), width))
        return carry

    lax.fori_loop(low, high, step, 0, unroll=6 if width == 256 else 2)


def columns(body):
    tiles(0, INNER // 256, lambda tile, cols: body(cols), 256)


def make_scores(s):
    masks = s.masks[...]
    ids_row = masks.T[IDS : IDS + 1]
    allowed = lower_triangle() & (masks[:, IDS : IDS + 1] == ids_row)
    s.allowed[...] = jnp.where(allowed, 1.0, 0.0)
    s.scores[...] = jnp.where(allowed, dot(s.bc[:, STATE:], s.bc[:, :STATE], 1, 1), 0.0)


def mix_inside(s, low, high):
    half = ROWS // 2

    def body(tile, cols):
        logs = pltpu.roll(s.logs[...], (128 - 2 * tile) % 128, 1)
        top, bottom = jnp.zeros((half, 128), F32), jnp.zeros((half, 128), F32)
        for j, vals in enumerate(pair(s.vals, cols, first_half())):
            h = 2 * tile + j
            column, row, dt = logs[:, j : j + 1], s.logs_t[pl.ds(h, 1), :], s.dt_t[pl.ds(h, 1), :]
            decay = (jnp.exp(jnp.minimum(column[:half] - row[:, :half], 0.0)) * dt[:, :half]).astype(BF16)
            s.dec[h, :half, :half] = decay
            mix = (s.scores[:half, :half] * decay.astype(F32)).astype(BF16)
            top = top + dot(mix, vals[:half], 1, 0)
            decay = (jnp.exp(jnp.minimum(column[half:] - row, 0.0)) * dt).astype(BF16)
            s.dec[h, half:, :] = decay
            mix = (s.scores[half:, :] * decay.astype(F32)).astype(BF16)
            bottom = bottom + dot(mix, vals, 1, 0)
        s.inner[:half, cols] = top
        s.inner[half:, cols] = bottom

    tiles(low, high, body)


def value_slopes(s):
    def body(cols):
        s.vsum[:, cols] = silu_slope(s.vsum[:, cols])

    columns(body)
    s.ssum[...] = silu_slope(s.ssum[...])


def gate_slopes(s):
    def body(cols):
        gate = s.gate[:, cols]
        sig = jax.nn.sigmoid(gate)
        silu = gate * sig
        s.gate[:, cols] = silu
        s.gslope[:, cols] = (sig + silu * (1.0 - sig)).astype(BF16)

    columns(body)


def add_states(s):
    top, rest = halves(s.masks[:, JOINED : JOINED + 1] * jnp.exp(s.logs[...]))
    s.weight_top2[...] = top
    s.weight_rest2[...] = rest
    unpack(s.state, s.state_in)
    s.skips[...] = to_units(s.skip[...], s.lanes[...])
    s.squares[...] = jnp.zeros_like(s.squares)

    def body(cols):
        carried = dot(s.weight_top2[...], s.lanes[:, cols], 1, 0) + dot(s.weight_rest2[...], s.lanes[:, cols], 1, 0)
        inner = s.inner[:, cols] + dot(s.bc[:, STATE:], s.state[:, cols], 1, 0) * carried
        s.inner[:, cols] = inner
        gated = (inner + s.skips[0:1, cols] * s.vals[:, cols].astype(F32)) * s.gate[:, cols]
        s.normal[:, cols] = gated
        s.squares[...] = s.squares[...] + gated * gated

    columns(body)


def gated_norm(s):
    inverse = lax.rsqrt(jnp.sum(s.squares[...], axis=1, keepdims=True) / INNER + EPSILON)
    s.inverse[...] = jnp.broadcast_to(inverse, (ROWS, 128))
    for t in range(PARTS):
        s.gain_out[:, of_part(t)] = jnp.broadcast_to(s.prm[t, 5:6, :WIDE], (8, WIDE))
    s.squares[...] = jnp.zeros_like(s.squares)

    def body(cols):
        normal = s.normal[:, cols] * s.inverse[:, 0:1]
        s.normal[:, cols] = normal
        gain = s.gain_out[0:1, cols]
        s.nout[:, cols] = (normal * gain).astype(BF16)
        d_out = s.dout[:, cols]
        product = d_out * normal
        s.small[5:6, cols] = jnp.sum(product, axis=0, keepdims=True)
        s.squares[...] = s.squares[...] + product * gain

    columns(body)


def project_back(s, t):
    cols = of_part(t)
    s.dout[:, cols] = dot(s.cot[...], weights_of(s.wg, t)[:, WIDE:], 1, 0)


def project_out(s):
    branch = s.x[...].astype(F32)
    for t in range(PARTS):
        branch = branch + dot(s.nout[:, of_part(t)], weights_of(s.wg, t)[:, WIDE:], 1, 1)
    s.result_in[...] = branch.astype(BF16)


def gated_norm_back(s):
    total = jnp.sum(s.squares[...], axis=1, keepdims=True) / INNER
    s.dots[...] = jnp.broadcast_to(total, (ROWS, 128))

    def body(cols):
        d_scaled = s.dout[:, cols] * s.gain_out[0:1, cols]
        d_gated = s.inverse[:, 0:1] * (d_scaled - s.normal[:, cols] * s.dots[:, 0:1])
        vals = s.vals[:, cols].astype(F32)
        mixed = s.inner[:, cols] + s.skips[0:1, cols] * vals
        d_mixed = d_gated * s.gate[:, cols]
        s.dgate[:, cols] = (d_gated * mixed * s.gslope[:, cols].astype(F32)).astype(BF16)
        s.small[6:7, cols] = jnp.sum(d_mixed * vals, axis=0, keepdims=True)
        s.dy[:, cols] = d_mixed.astype(BF16)
        s.dval[:, cols] = s.skips[0:1, cols] * d_mixed
        lanes = s.lanes[:, cols]
        carried = dot(s.weight_top2[...], lanes, 1, 0) + dot(s.weight_rest2[...], lanes, 1, 0)
        d_carried = (d_mixed * carried).astype(BF16)
        s.dcar[:, cols] = d_carried
        s.dfresh[:, cols] = dot(s.bc[:, STATE:], d_carried, 0, 0).astype(BF16)

    columns(body)


def states_back(s):
    pack(s.dstate, s.dfresh)


def mix_back(s, low, high):
    half = ROWS // 2

    def body(tile, cols):
        total = jnp.zeros((ROWS, 128), F32)
        top, bottom = s.dscores[:half, :half], s.dscores[half:, :]
        blank = jnp.zeros((half, half), BF16)
        first = first_half()
        for j, (vals, grads) in enumerate(zip(pair(s.vals, cols, first), pair(s.dy, cols, first))):
            h = 2 * tile + j
            decay = s.dec[h, :half, :half].astype(F32)
            top = top + dot(grads[:half], vals[:half], 1, 1) * decay
            above = (s.scores[:half, :half] * decay).astype(BF16)
            decay = s.dec[h, half:, :].astype(F32)
            bottom = bottom + dot(grads[half:], vals, 1, 1) * decay
            below = (s.scores[half:, :] * decay).astype(BF16)
            mix = jnp.concatenate([jnp.concatenate([above, blank], axis=1), below], axis=0)
            total = total + dot(mix, grads, 0, 0)
        s.dscores[:half, :half] = top
        s.dscores[half:, :] = bottom
        s.dval[:, cols] = s.dval[:, cols] + total
        s.dout[:, cols] = total * s.vals[:, cols].astype(F32)

    tiles(low, high, body)


def after_mix_back(s):
    s.direct[...] = jnp.zeros_like(s.direct)
    s.dlog[...] = jnp.zeros_like(s.dlog)

    def body(cols):
        lanes = s.lanes[:, cols]
        from_values = s.dout[:, cols]
        s.direct[...] = s.direct[...] + to_heads(from_values, lanes)
        s.dlog[...] = s.dlog[...] + to_heads(s.dy[:, cols].astype(F32) * s.inner[:, cols] - from_values, lanes)

    columns(body)
    d_scores = (s.dscores[...] * s.allowed[...]).astype(BF16)
    s.dbc[:, :STATE] = dot(d_scores, s.bc[:, STATE:], 0, 0)
    s.dbc[:, STATE:] = dot(d_scores, s.bc[:, :STATE], 1, 0) + dot(s.dcar[...], s.state[...], 1, 1)


def leave(s):
    lanes = s.lanes[...]
    logs, dt, raw, masks = s.logs[...], s.dt[...], s.raw[...], s.masks[...]
    unpack(s.coming, s.coming_in)
    last = logs[ROWS - 1 :]
    s.through[...] = jnp.zeros_like(s.through)

    def body(cols):
        lanes = s.lanes[:, cols]
        weights = dot(s.weight_top[...], lanes, 1, 0) + dot(s.weight_rest[...], lanes, 1, 0)
        weighted = s.vals[:, cols].astype(F32) * weights
        below = dot(s.bc[:, :STATE], s.coming[:, cols], 1, 0)
        s.dsum[:ROWS, cols] = (s.dval[:, cols] + weights * below) * s.vsum[:, cols]
        s.through[...] = s.through[...] + to_heads(weighted * below, lanes)
        s.dbc[:, :STATE] = s.dbc[:, :STATE] + dot(weighted.astype(BF16), s.coming[:, cols], 1, 1)

    columns(body)
    through, coming = s.through[...], s.coming[...]
    kept = masks[0:8, KEPT : KEPT + 1] * jnp.exp(jnp.broadcast_to(last, (8, 128)))
    held = jnp.sum(coming.astype(F32) * s.state[...].astype(F32), axis=0, keepdims=True)
    d_kept = to_heads(jnp.broadcast_to(held, (8, INNER)), lanes)
    d_last = jnp.sum(through, axis=0, keepdims=True) + (d_kept * kept)[0:1]
    row = lax.broadcasted_iota(jnp.int32, (ROWS, ROWS), 0)
    upper = row <= lax.broadcasted_iota(jnp.int32, (ROWS, ROWS), 1)
    d_rate = dot(upper.astype(F32), s.dlog[...] - through, 1, 0, HIGHEST) + d_last
    by_rate = dt * s.rate[0:1] * d_rate
    slope = jnp.where(raw < -15.0, 1.0, jax.nn.sigmoid(raw) / jnp.where(raw < -15.0, 1.0, dt))
    is_head = lax.broadcasted_iota(jnp.int32, (ROWS, 128), 1) < HEADS
    d_step = jnp.where(is_head, (s.direct[...] + through + by_rate) * slope, 0.0)
    s.dstep[...] = d_step.astype(BF16)
    s.small[7:8, 0:128] = jnp.sum(d_step, axis=0, keepdims=True)
    s.small[7:8, 128:256] = jnp.sum(by_rate, axis=0, keepdims=True)
    s.dsum[:ROWS, INNER:] = s.dbc[...] * s.ssum[...]
    s.edge[...] = s.dsum[0:8]


def conv_grads(s):
    masks = s.masks[...]

    def rows_of(d_sum, before_ref, cols):
        rows = []
        for k in (3, 2, 1):
            shifted = masks[:, SAME + k : SAME + k + 1] * before_ref[HALO - k : HALO - k + ROWS, cols]
            rows.append(jnp.sum(d_sum * shifted, axis=0, keepdims=True))
        rows.append(jnp.sum(d_sum * before_ref[HALO:, cols], axis=0, keepdims=True))
        rows.append(jnp.sum(d_sum, axis=0, keepdims=True))
        return rows

    def body(cols):
        for k, row in enumerate(rows_of(s.dsum[:ROWS, cols], s.vpre, cols)):
            s.small[k : k + 1, cols] = row

    columns(body)
    for k, row in enumerate(rows_of(s.dsum[:ROWS, INNER:], s.spre, EVERY)):
        s.small[7:8, 256 * (k + 1) : 256 * (k + 2)] = row


def conv_back(s):
    masks = s.masks[...]

    def back(cols, taps):
        total = taps[3:4] * s.dsum[:ROWS, cols]
        for k in (1, 2, 3):
            ahead = masks[:, AFTER + k : AFTER + k + 1] * s.dsum[k : k + ROWS, cols]
            total = total + taps[3 - k : 4 - k] * ahead
        return total.astype(BF16)

    for t in range(PARTS):
        cols = of_part(t)
        s.dvlow[:, cols] = back(cols, s.prm[t, 0:4, :WIDE])
    s.dshared[...] = back(slice(INNER, INNER + 2 * STATE), s.conv_shared[...])


def as_block(v):
    return v.reshape(4, 2, 2, 3, 16, v.shape[-1])


def parts_g(s, t):
    cols = of_part(t)
    gates = dot(s.normed_t[...], s.dgate[:, cols], 1, 0)
    outs = dot(s.cot_t[...], s.nout[:, cols], 1, 0)
    s.pg[t // 4, t % 4] = as_block(jnp.concatenate([gates, outs], axis=1).astype(BF16))


def parts_shared(s):
    shared = dot(s.normed_t[...], s.dshared[...], 1, 0)
    blank = jnp.zeros((4, 128), F32)
    for k in range(128):
        strip = shared[k // 2 * 12 : k // 2 * 12 + 12, k % 2 * 128 : k % 2 * 128 + 128]
        s.ps[k // 32, k // 16 % 2, k // 8 % 2, k % 8] = jnp.concatenate([strip, blank], axis=0).astype(BF16)


def parts_v(s):
    steps = dot(s.normed_t[...], s.dstep[...], 1, 0)[:, :64].astype(BF16)
    for t in range(PARTS):
        values = dot(s.normed_t[...], s.dvlow[:, of_part(t)], 1, 0).astype(BF16)
        s.pv[t // 4, t % 4] = as_block(jnp.concatenate([values, steps], axis=1))


def normed_back_g(s):
    total = jnp.zeros((ROWS, D), F32)
    for t in range(PARTS):
        total = total + dot(s.dgate[:, of_part(t)], weights_of(s.wg, t)[:, :WIDE], 1, 1)
    s.dnormed[...] = total


def normed_back_v(s):
    total = s.dnormed[...] + dot(s.dshared[...], s.w_shared[...], 1, 1)
    total = total + dot(pltpu.roll(s.dstep[...].astype(F32), 64, 1).astype(BF16), s.wstep[...], 1, 1)
    for t in range(PARTS):
        total = total + dot(s.dvlow[:, of_part(t)], weights_of(s.wv, t)[:, :WIDE], 1, 1)
    x = s.x[...].astype(F32)
    inverse = lax.rsqrt(jnp.mean(x * x, axis=1, keepdims=True) + EPSILON)
    scaled = x * inverse
    d_in = total * s.in_gain[...].reshape(1, D)
    gains = jnp.sum(total * scaled, axis=0, keepdims=True)
    s.gain_row[...] = jnp.zeros_like(s.gain_row)
    for k in range(D // 128):
        s.gain_row[k : k + 1] = gains[:, k * 128 : k * 128 + 128]
    centred = jnp.mean(d_in * scaled, axis=1, keepdims=True)
    s.resid_in[...] = inverse * (d_in - scaled * centred) + s.cot[...].astype(F32)


def own_part(row, me, width):
    total = jnp.where(me["t"] == 0, row[:, :width], 0.0)
    for t in range(1, PARTS):
        total = total + jnp.where(me["t"] == t, row[:, t * width : (t + 1) * width], 0.0)
    return total


def closing_kernel(*refs):
    names = [*RESULTS, *OUTPUTS]
    s = types.SimpleNamespace(**dict(zip(names, refs)))
    me = place()
    s.result[...] = s.result_in[...]
    s.grad_resid[...] = s.resid_in[...]
    s.grad_w_value[...] = s.block_v[:, :WIDE]
    steps = s.block_v[:, 128:].T
    s.grad_w_step[...] = sum(jnp.where(me["t"] == t, steps[64 + 3 * t : 67 + 3 * t], 0.0) for t in range(PARTS))
    s.grad_w_gate[...] = s.block_g[:, :WIDE]
    s.grad_w_out[...] = s.block_g[:, WIDE:]
    total = s.total[...]
    own = own_part(total, me, WIDE)
    s.grad_conv_inner[...] = own[0:4]
    s.grad_bias_inner[...] = own[4:5].reshape(WIDE)
    s.grad_out_gain[...] = own[5:6].reshape(WIDE)
    for k in range(4):
        s.grad_conv_shared[k : k + 1] = total[7:8, 256 * (k + 1) : 256 * (k + 2)]
    s.grad_bias_shared[...] = total[7:8, 1280:].reshape(2 * STATE)
    s.grad_step_bias[...] = own_part(total[7:8, 0:24], me, 3)
    s.grad_decay_log[...] = own_part(total[7:8, 128:152], me, 3)
    s.grad_skip_gain[...] = own_part(to_heads(total, head_lanes())[6:7, 0:24], me, 3)
    for k in range(D // 128):
        s.grad_in_gain[k * 128 : k * 128 + 128] = s.gains[k]
    for k in range(128):
        tile = s.tails_in[k // 32, k // 16 % 2, k // 8 % 2, k % 8].astype(F32)
        s.grad_w_shared[k // 2 * 12 : k // 2 * 12 + 12, k % 2 * 128 : k % 2 * 128 + 128] = tile[:12]


INPUTS = dict(
    x=0, cot=0, segs=0, in_gain=0, w_gate=0, w_value=0, w_step=0, w_shared=0, conv_inner=0, bias_inner=0,
    conv_shared=0, bias_shared=0, step_bias=1, decay_log=1, skip_gain=1, out_gain=0, w_out=0,
)
OUTPUTS = dict(
    result=((ROWS, D), BF16), grad_resid=((ROWS, D), F32), grad_in_gain=((D,), F32),
    grad_w_gate=((48, WIDE), F32), grad_w_value=((48, WIDE), F32), grad_w_step=((3, 48), F32),
    grad_w_shared=((D, 2 * STATE), F32), grad_conv_inner=((4, WIDE), F32), grad_bias_inner=((WIDE,), F32),
    grad_conv_shared=((4, 2 * STATE), F32), grad_bias_shared=((2 * STATE,), F32),
    grad_step_bias=((1, 3), F32), grad_decay_log=((1, 3), F32), grad_skip_gain=((1, 3), F32),
    grad_out_gain=((WIDE,), F32), grad_w_out=((48, WIDE), F32),
)
RESULTS = dict(
    result_in=((ROWS, D), BF16), resid_in=((ROWS, D), F32), block_v=((48, PACK_V), F32),
    block_g=((48, PACK_G), F32), total=((8, INNER), F32), gains=((8, 128), F32),
    tails_in=((4, 2, 2, 8, 16, 128), BF16),
)
TORUS = (2, 4, 4, 2, 2, 3, 16)


def reduce_scratch(width, relayed, orders):
    block = (16, width)
    last = [free_shape(order[2:]) + block for order in orders]
    half = [free_shape(order[2:], True) + block for order in orders]
    line = [free_shape(order[1:]) + block for order in orders]
    kinds = [(4, last), (2 if relayed else 3, last), (3, line)]
    shapes = [(lead,) + shape for lead, shapes in kinds for shape in shapes] + [(3, 3) + block]
    return shapes + ([(2,) + shape for shape in half] if relayed else [])


SCRATCH = dict(
    wv=(TORUS + (PACK_V,), BF16), wg=(TORUS + (PACK_G,), BF16),
    pv=(TORUS + (PACK_V,), BF16), pg=(TORUS + (PACK_G,), BF16), ps=((4, 2, 2, 8, 16, 128), BF16), heard_s=((4, 2, 8, 16, 128), BF16),
    got_s=((64, 16, 128), BF16),
    own_v=((3, 16, PACK_V), BF16), own_g=((3, 16, PACK_G), BF16), own_t=((16, 128), BF16), turned=((64, 128), F32),
    own_p=((8, 256), F32), prm=((PARTS, 8, 256), F32), ahead=((HALO, D), BF16),
    normed=((HALO + ROWS, D), BF16), normed_t=((D, ROWS), BF16), cot_t=((D, ROWS), BF16),
    masks=((ROWS, 128), F32), lanes=((128, INNER), BF16), dfresh=((STATE, INNER), BF16),
    weight_top=((ROWS, 128), BF16), weight_rest=((ROWS, 128), BF16), through=((ROWS, 128), F32),
    weight_top2=((ROWS, 128), BF16), weight_rest2=((ROWS, 128), BF16), dots=((ROWS, 128), F32),
    squares=((ROWS, 256), F32),
    vpre=((HALO + ROWS, INNER), F32), vsum=((ROWS, INNER), F32), vals=((ROWS, INNER), BF16),
    spre=((HALO + ROWS, 256), F32), ssum=((ROWS, 256), F32), bc=((ROWS, 256), BF16),
    rate=((8, 128), F32), skip=((8, 128), F32), skips=((8, INNER), F32), gain_out=((8, INNER), F32),
    wstep=((D, 128), BF16), raw=((ROWS, 128), F32), dt=((ROWS, 128), F32), logs=((ROWS, 128), F32),
    dt_t=((128, ROWS), F32), logs_t=((128, ROWS), F32),
    fresh=((PARTS, 208, 128), BF16), fresh_in=((PARTS, 208, 128), BF16),
    state_out=((PARTS, STATE + 64, 128), BF16), state_in=((PARTS, STATE + 64, 128), BF16),
    dstate=((PARTS, STATE + 64, 128), BF16), dstate_in=((PARTS, STATE + 64, 128), BF16),
    coming_out=((PARTS, STATE + 64, 128), BF16), coming_in=((PARTS, STATE + 64, 128), BF16),
    state=((STATE, INNER), BF16),
    scores=((ROWS, ROWS), F32), dscores=((ROWS, ROWS), F32), allowed=((ROWS, ROWS), F32),
    dec=((HEADS, ROWS, ROWS), BF16),
    inner=((ROWS, INNER), F32),
    gate=((ROWS, INNER), F32), gslope=((ROWS, INNER), BF16), normal=((ROWS, INNER), F32),
    inverse=((ROWS, 128), F32), nout=((ROWS, INNER), BF16), dout=((ROWS, INNER), F32),
    dgate=((ROWS, INNER), BF16), dy=((ROWS, INNER), BF16), dcar=((ROWS, INNER), BF16),
    direct=((ROWS, 128), F32), dlog=((ROWS, 128), F32),
    dbc=((ROWS, 256), F32), dstep=((ROWS, 128), BF16),
    dsum=((ROWS + 8, INNER + 256), F32), edge=((8, INNER + 256), F32),
    dshared=((ROWS, 256), BF16),
    small=((8, INNER), F32), small_sums=((4, 8, INNER), F32), small_got=((10, 8, INNER), F32),
    gain_row=((8, 128), F32), gain_sums=((4, 8, 128), F32), gain_got=((10, 8, 128), F32),
)
SEMAPHORES = dict(
    gather_v=45, gather_g=45, shared=4, reduce_g=42, reduce_v=42,
    total=10, total_gain=10, swap_p=8, swap1=8, swap2=8, swap3=8, swap4=8, edges=2,
)


def reducer(me, orders, parts, refs, sems):
    return Reduce(me, orders, parts, refs[0:3], refs[10:13] or None, refs[3:6], refs[6:9], refs[9], sems)


REDUCE_G = reduce_scratch(PACK_G, True, ASIDE)
REDUCE_V = reduce_scratch(PACK_V, False, ORDERS)


def everything(s, sems):
    me = place()
    dp, t = me["dp"], me["t"]
    after, before = (dp, (t + 1) % PARTS), (dp, (t + 7) % PARTS)
    greet(me)
    make_blocks(s, me)
    in_gain = s.in_gain[...].reshape(1, D)
    s.normed[HALO:] = norm_of(s.x[...], in_gain)
    make_masks(s, me)
    greeted()

    gather_v = Gather(me, s.own_v, s.wv, sems.gather_v, False)
    gather_g = Gather(me, s.own_g, s.wg, sems.gather_g, True)
    gather_v.first()
    halo = transfer(s.x.at[pl.ds(ROWS - HALO, HALO)], s.ahead, sems.edges, 0, after)
    gather_g.first()
    params = [transfer(s.own_p, s.prm.at[t], sems.swap_p, by, (dp, (t + by) % PARTS)) for by in range(1, PARTS)]
    s.prm[t] = s.own_p[...]
    s.lanes[...] = head_lanes()
    gather_v.second()
    halo.wait_recv()
    s.normed[:HALO] = norm_of(s.ahead[...], in_gain)
    gather_v.third()
    gather_g.second()
    enter_shared(s)
    make_scores(s)
    s.normed_t[...] = s.normed[HALO:].T
    s.cot_t[...] = s.cot[...].T
    for copy in params:
        copy.wait_recv()
    gather_v.relay()
    gather_v.finish()
    gather_g.third()
    gather_v.settle()

    enter_step(s)
    for part in range(PARTS):
        enter_value(s, part)
    make_fresh(s)
    swap1 = Swap(me, s.fresh, s.fresh_in, sems.swap1)
    swap1.start()
    mix_inside(s, 0, 4)
    gather_g.relay()
    mix_inside(s, 4, 10)
    value_slopes(s)
    gather_v.drain()
    swap1.wait()
    scan_states(s)
    swap2 = Swap(me, s.state_out, s.state_in, sems.swap2)
    swap2.start()
    gather_g.finish()
    mix_inside(s, 10, 12)
    gather_g.settle()
    for part in range(PARTS):
        s.gate[:, of_part(part)] = dot(s.normed[HALO:], weights_of(s.wg, part)[:, :WIDE], 1, 0)
        project_back(s, part)
    gate_slopes(s)
    swap1.drain()
    for copy in [halo, *params]:
        copy.wait_send()
    gather_g.drain()
    swap2.wait()
    add_states(s)
    gated_norm(s)
    gated_norm_back(s)
    states_back(s)
    swap3 = Swap(me, s.dstate, s.dstate_in, sems.swap3)
    swap3.start()
    for part in range(PARTS):
        parts_g(s, part)
    reduce_g = reducer(me, ASIDE, s.pg, s.refs_g, sems.reduce_g)
    reduce_g.swap()
    s.dscores[...] = jnp.zeros_like(s.dscores)
    project_out(s)
    mix_back(s, 0, 2)
    reduce_g.relay()
    mix_back(s, 2, 6)
    swap2.drain()
    swap3.wait()
    scan_back(s)
    swap4 = Swap(me, s.coming_out, s.coming_in, sems.swap4)
    swap4.start()
    mix_back(s, 6, 8)
    reduce_g.third()
    mix_back(s, 8, 12)
    after_mix_back(s)
    normed_back_g(s)
    swap3.drain()
    swap4.wait()
    leave(s)
    edge = transfer(s.edge, s.dsum.at[pl.ds(ROWS, 8)], sems.edges, 1, before)
    conv_grads(s)
    swap4.drain()
    total = Total(me, s.small, s.small_sums, s.small_got, sems.total)
    total.along(0)
    reduce_g.second()
    edge.wait_recv()
    total.add(0)
    total.along(1)
    conv_back(s)
    parts_shared(s)
    shared = Shared(me, s.ps, s.heard_s, s.got_s, s.own_t, s.tails_in, sems.shared)
    shared.swap()
    parts_v(s)
    reduce_v = reducer(me, ORDERS, s.pv, s.refs_v, sems.reduce_v)
    reduce_v.swap()
    shared.scatter()
    total.add(1)
    total.along(2)
    reduce_v.relay()
    reduce_v.third()
    normed_back_v(s)
    gain = Total(me, s.gain_row, s.gain_sums, s.gain_got, sems.total_gain)
    gain.along(0)
    reduce_g.first()
    shared.gather()
    gain.add(0)
    gain.along(1)
    total.add(2)
    total.along(3)
    reduce_v.second()
    gain.add(1)
    gain.along(2)
    reduce_v.first()
    gain.add(2)
    gain.along(3)
    shared.share()
    for p in range(3):
        s.block_g[16 * p : 16 * p + 16] = reduce_g.result(p)
    for p in range(3):
        s.block_v[16 * p : 16 * p + 16] = reduce_v.result(p)
    total.add(3)
    s.total[...] = s.small_sums[3]
    gain.add(3)
    s.gains[...] = s.gain_sums[3]
    shared.finish()

    for channel in (shared, reduce_g, reduce_v, total, gain):
        channel.drain()
    edge.wait_send()


def kernel(*refs):
    tables = (INPUTS, RESULTS, SCRATCH)
    names = [name for table in tables for name in table]
    s = types.SimpleNamespace(**dict(zip(names, refs)))
    s.dval, s.dvlow = s.normal, s.dy
    s.dnormed, s.coming = s.gate.at[:, :D], s.dcar.at[:STATE]
    at = len(names)
    s.refs_g, at = refs[at : at + len(REDUCE_G)], at + len(REDUCE_G)
    s.refs_v, at = refs[at : at + len(REDUCE_V)], at + len(REDUCE_V)
    pairs = zip(refs[at::2], refs[at + 1 :: 2])
    everything(s, types.SimpleNamespace(**dict(zip(SEMAPHORES, pairs))))


def shards(*args):
    args = list(args)
    args[6] = args[6].T
    vmem, smem = pl.BlockSpec(memory_space=pltpu.VMEM), pl.BlockSpec(memory_space=pltpu.SMEM)
    scratch = [pltpu.VMEM(shape, dtype) for shape, dtype in SCRATCH.values()]
    scratch += [pltpu.VMEM(shape, BF16) for shape in REDUCE_G + REDUCE_V]
    for count in SEMAPHORES.values():
        scratch += [pltpu.SemaphoreType.DMA((count,)), pltpu.SemaphoreType.DMA((count,))]
    shapes = lambda table: tuple(jax.ShapeDtypeStruct(shape, dtype) for shape, dtype in table.values())
    results = pl.pallas_call(
        kernel,
        out_shape=shapes(RESULTS),
        in_specs=[smem if scalar else vmem for scalar in INPUTS.values()],
        out_specs=tuple(vmem for _ in RESULTS),
        scratch_shapes=scratch,
        compiler_params=pltpu.CompilerParams(
            collective_id=0, has_side_effects=True, vmem_limit_bytes=VMEM_LIMIT
        ),
    )(*args)
    outs = pl.pallas_call(
        closing_kernel,
        out_shape=shapes(OUTPUTS),
        in_specs=[vmem for _ in RESULTS],
        out_specs=tuple(vmem for _ in OUTPUTS),
    )(*results)
    outs = [out.reshape(3) if out.shape == (1, 3) else out for out in outs]
    outs[5] = outs[5].T
    return tuple(outs)


def solution(mesh):
    rows, cols = P(("dp", "tensor"), None), P("dp", "tensor")
    head, whole = P("tensor"), P()
    in_specs = (
        rows, rows, P("dp"), whole, cols, cols, cols, whole, P(None, "tensor"), head,
        whole, whole, head, head, head, head, cols,
    )
    out_specs = (
        rows, rows, whole, cols, cols, cols, whole, P(None, "tensor"), head,
        whole, whole, head, head, head, head, cols,
    )
    return jax.shard_map(shards, mesh=mesh, in_specs=in_specs, out_specs=out_specs, check_vma=False)
```
